32 devices in a mesh: img: 8 (over z, core), txt: 4 (over y, x).
Axes of the slice: x: 2, y: 2, z: 4, core: 2. Of those that a mesh axis runs over, the one named last changes fastest.
Arguments:
- image_feats: bfloat16 [512, 768], P(('img', 'txt')), may hold values from -6 to 6
- text_feats: bfloat16 [512, 512], P(('txt', 'img')), may hold values from -6 to 6
- teacher_img: bfloat16 [512, 1024], P(('img', 'txt')), may hold values from -60 to 60, as said below
- teacher_txt: bfloat16 [512, 1024], P(('txt', 'img')), may hold values from -60 to 60, as said below
- proj_img: bfloat16 [768, 512], replicated, may hold values from -0.21875 to 0.21875
- proj_txt: bfloat16 [512, 512], replicated, may hold values from -0.25 to 0.25
Outputs:
- loss: float32 [], replicated
- grad_img: float32 [768, 512], replicated
- grad_txt: float32 [512, 512], replicated
The draws below stay inside these ranges and needn't reach their ends.
Inputs may be any that keep to these rules, and one draw needn't show every extreme that they name: `teacher_img`: raw teacher embeddings, rows of various scales. `teacher_txt`: raw teacher embeddings, rows of various scales.
All inputs are finite; a program needn't handle non-finite values.
Results may differ from the reference program's by a relative error of at most 0.0077.
Values may be sent and summed in bfloat16 or wider, within the bound.
A program may use at most 64 MiB of HBM per device.

```python
import jax
import jax.numpy as jnp
from jax import lax

DT = 1024
DS = 512
FI = 768
FT = 512
BATCH = 512


def teacher_rows(key, own_key):
    scale_key = jax.random.fold_in(own_key, 5)
    scales = jnp.exp(jax.random.uniform(scale_key, (BATCH, 1), jnp.float32, 0.0, jnp.log(10.0)))
    own = jax.random.truncated_normal(own_key, -4.0, 4.0, (BATCH, DT), jnp.float32)
    return (own * scales).astype(jnp.bfloat16)


def draw_teacher_img(key, part):
    own_key = jax.random.fold_in(key, 11)
    return teacher_rows(key, own_key)


def draw_teacher_txt(key, part):
    own_key = jax.random.fold_in(key, 12)
    return teacher_rows(key, own_key)


def level_of(rng, extent, pieces, least, largest):
    gain = 1.0
    for axis_at, blocks in pieces:
        steps = jax.random.uniform(jax.random.fold_in(jax.random.fold_in(rng, 6), axis_at), (blocks,), jnp.float32, least / len(pieces), largest / len(pieces))
        gain = gain * jnp.repeat(jnp.exp(steps), extent[axis_at] // blocks).reshape((-1,) + (1,) * (len(extent) - 1 - axis_at))
    return gain


def noise(key, shape, scale, bound, split=(), kind=jnp.bfloat16):
    values = jax.random.normal(key, shape, jnp.float32) * scale
    if len(split) > 0:
        values = level_of(key, shape, split, -0.22, 0.18) * values
    return jnp.clip(values, min=-bound, max=bound).astype(kind)


def setup_inputs(seed: int = 0) -> dict:
    streams_of = jax.random.split(jax.random.key(seed), 7)
    return {
        "image_feats": noise(streams_of[0], (BATCH, FI), 1.0, 6.0, ((0, 32),)),
        "text_feats": noise(streams_of[1], (BATCH, FT), 1.0, 6.0, ((0, 32),)),
        "teacher_img": draw_teacher_img(jax.random.fold_in(streams_of[6], 71), 0),
        "teacher_txt": draw_teacher_txt(jax.random.fold_in(streams_of[6], 71), 0),
        "proj_img": noise(streams_of[4], (FI, DS), FI ** -0.5, 0.21875),
        "proj_txt": noise(streams_of[5], (FT, DS), FT ** -0.5, 0.25),
    }


EPS = 1e-06
TEACHER_SCALE = 100.0
STUDENT_SCALE = 50.0

def project(feats, weight):
    u = jnp.dot(feats, weight, preferred_element_type=jnp.float32)
    inv = lax.rsqrt(lax.optimization_barrier(jnp.sum(u * u, axis=1, keepdims=True)) + EPS)
    return (u * inv, inv)

def normed(raw):
    x = raw.astype(jnp.float32)
    return (x * lax.rsqrt(lax.optimization_barrier(jnp.sum(x * x, axis=1, keepdims=True)) + EPS)).astype(jnp.bfloat16)

def reference(image_feats, text_feats, teacher_img, teacher_txt, proj_img, proj_txt):
    e_img, inv_img = project(image_feats, proj_img)
    e_txt, inv_txt = project(text_feats, proj_txt)
    s_img = e_img.astype(jnp.bfloat16)
    s_txt = e_txt.astype(jnp.bfloat16)
    q_img = normed(teacher_img)
    q_txt = normed(teacher_txt)
    block = min(1024, BATCH)
    count = BATCH // block

    def tiles(k):
        start = (k * block).astype(jnp.int32)
        qb = lax.dynamic_slice_in_dim(q_img, start, block, 0)
        sb = lax.dynamic_slice_in_dim(s_img, start, block, 0)
        tl = TEACHER_SCALE * jnp.dot(qb, q_txt.T, preferred_element_type=jnp.float32)
        sl = STUDENT_SCALE * jnp.dot(sb, s_txt.T, preferred_element_type=jnp.float32)
        return (tl, sl, sb)

    def col_step(carry, k):
        tm, ts, sm, ss = carry
        tl, sl, sb = tiles(k)
        tm2 = jnp.maximum(tm, tl.max(0))
        sm2 = jnp.maximum(sm, sl.max(0))
        ts2 = ts * jnp.exp(tm - tm2) + lax.optimization_barrier(jnp.sum(jnp.exp(tl - tm2[None, :]), 0))
        ss2 = ss * jnp.exp(sm - sm2) + lax.optimization_barrier(jnp.sum(jnp.exp(sl - sm2[None, :]), 0))
        return ((tm2, ts2, sm2, ss2), None)
    low = jnp.full((BATCH,), -jnp.inf, jnp.float32)
    zero = jnp.zeros((BATCH,), jnp.float32)
    (ctm, cts, csm, css), _ = lax.scan(col_step, (low, zero, low, zero), jnp.arange(count, dtype=jnp.int32))

    def grad_step(carry, k):
        acc_txt, total = carry
        tl, sl, sb = tiles(k)
        rtm = tl.max(1)
        rsm = sl.max(1)
        et_row = jnp.exp(tl - rtm[:, None])
        es_row = jnp.exp(sl - rsm[:, None])
        rts = lax.optimization_barrier(jnp.sum(et_row, 1))
        rss = lax.optimization_barrier(jnp.sum(es_row, 1))
        pt_row = et_row / rts[:, None]
        ps_row = es_row / rss[:, None]
        pt_col = jnp.exp(tl - ctm[None, :]) / cts[None, :]
        ps_col = jnp.exp(sl - csm[None, :]) / css[None, :]
        diff = tl - sl
        term = jnp.sum(pt_row * diff) + jnp.sum(pt_col * diff)
        term = term + jnp.sum(rsm + jnp.log(rss) - rtm - jnp.log(rts))
        grad_tile = (0.5 * STUDENT_SCALE * (ps_row - pt_row + (ps_col - pt_col))).astype(jnp.bfloat16)
        d_img = jnp.dot(grad_tile, s_txt, preferred_element_type=jnp.float32)
        acc_txt = acc_txt + lax.dot_general(grad_tile, sb, (((0,), (0,)), ((), ())), preferred_element_type=jnp.float32)
        return ((acc_txt, total + term), d_img)
    init = (jnp.zeros((BATCH, DS), jnp.float32), jnp.zeros((), jnp.float32))
    (d_txt, total), d_blocks = lax.scan(grad_step, init, jnp.arange(count, dtype=jnp.int32))
    d_img = d_blocks.reshape(BATCH, DS)
    total = total + jnp.sum(csm + jnp.log(css) - ctm - jnp.log(cts))
    du_img = (d_img - e_img * lax.optimization_barrier(jnp.sum(e_img * d_img, 1, keepdims=True))) * inv_img
    du_txt = (d_txt - e_txt * lax.optimization_barrier(jnp.sum(e_txt * d_txt, 1, keepdims=True))) * inv_txt
    grad_img = jnp.dot(image_feats.astype(jnp.float32).T, du_img, precision=lax.Precision.HIGHEST)
    grad_txt = jnp.dot(text_feats.astype(jnp.float32).T, du_txt, precision=lax.Precision.HIGHEST)
    loss = total / (2.0 * BATCH)
    return (loss, grad_img, grad_txt)
```

```python
import functools

import jax
import jax.numpy as jnp
from jax import lax
from jax.experimental import pallas as pl
from jax.experimental.pallas import tpu as pltpu
from jax.sharding import PartitionSpec as P

EPS = 1e-06
TEACHER_SCALE = 100.0
STUDENT_SCALE = 50.0


def project(feats, weight):
    u = jnp.dot(feats, weight, preferred_element_type=jnp.float32)
    inv = lax.rsqrt(jnp.sum(u * u, axis=1, keepdims=True) + EPS)
    return (u * inv, inv)


def normed(raw):
    x = raw.astype(jnp.float32)
    return (x * lax.rsqrt(jnp.sum(x * x, axis=1, keepdims=True) + EPS)).astype(jnp.bfloat16)


def tangent(grad_rows, embeds, inverse):
    return (grad_rows - embeds * jnp.sum(embeds * grad_rows, 1, keepdims=True)) * inverse


def weight_grad(feats, du_rows):
    return lax.dot_general(
        feats.astype(jnp.float32),
        du_rows,
        (((0,), (0,)), ((), ())),
        precision=lax.Precision.HIGHEST,
    )


def tile_terms(block_q_img, block_q_txt, block_s_img, block_s_txt):
    tl = TEACHER_SCALE * jnp.dot(block_q_img, block_q_txt.T, preferred_element_type=jnp.float32)
    sl = STUDENT_SCALE * jnp.dot(block_s_img, block_s_txt.T, preferred_element_type=jnp.float32)
    rtm, rsm = lax.pmax((tl.max(1), sl.max(1)), "txt")
    rts, rss = lax.psum(
        (jnp.sum(jnp.exp(tl - rtm[:, None]), 1), jnp.sum(jnp.exp(sl - rsm[:, None]), 1)), "txt"
    )
    ctm, csm = lax.pmax((tl.max(0), sl.max(0)), "img")
    cts, css = lax.psum(
        (jnp.sum(jnp.exp(tl - ctm[None, :]), 0), jnp.sum(jnp.exp(sl - csm[None, :]), 0)), "img"
    )
    pt_row = jnp.exp(tl - rtm[:, None]) / rts[:, None]
    ps_row = jnp.exp(sl - rsm[:, None]) / rss[:, None]
    pt_col = jnp.exp(tl - ctm[None, :]) / cts[None, :]
    ps_col = jnp.exp(sl - csm[None, :]) / css[None, :]
    diff = tl - sl
    n_img = lax.axis_size("img")
    n_txt = lax.axis_size("txt")
    local_term = jnp.sum(pt_row * diff) + jnp.sum(pt_col * diff)
    local_term = local_term + jnp.sum(rsm + jnp.log(rss) - rtm - jnp.log(rts)) / n_txt
    local_term = local_term + jnp.sum(csm + jnp.log(css) - ctm - jnp.log(cts)) / n_img
    grad_tile = (0.5 * STUDENT_SCALE * (ps_row - pt_row + (ps_col - pt_col))).astype(jnp.bfloat16)
    part_img = jnp.dot(grad_tile, block_s_txt, preferred_element_type=jnp.float32)
    part_txt = lax.dot_general(
        grad_tile, block_s_img, (((0,), (0,)), ((), ())), preferred_element_type=jnp.float32
    )
    return (part_img, part_txt, local_term)


def shards(image_feats, text_feats, teacher_img, teacher_txt, proj_img, proj_txt):
    e_img, inv_img = project(image_feats, proj_img)
    e_txt, inv_txt = project(text_feats, proj_txt)
    q_img = normed(teacher_img)
    q_txt = normed(teacher_txt)
    feats_img, block_q_img = (
        lax.all_gather(image_feats, "txt", axis=0, tiled=True),
        lax.all_gather(q_img, "txt", axis=0, tiled=True),
    )
    feats_txt, block_q_txt = (
        lax.all_gather(text_feats, "img", axis=0, tiled=True),
        lax.all_gather(q_txt, "img", axis=0, tiled=True),
    )
    block_s_img = project(feats_img, proj_img)[0].astype(jnp.bfloat16)
    block_s_txt = project(feats_txt, proj_txt)[0].astype(jnp.bfloat16)
    part_img, part_txt, local_term = tile_terms(block_q_img, block_q_txt, block_s_img, block_s_txt)
    d_img = lax.psum_scatter(part_img, "txt", scatter_dimension=0, tiled=True)
    d_txt = lax.psum_scatter(part_txt, "img", scatter_dimension=0, tiled=True)
    local_img = weight_grad(image_feats, tangent(d_img, e_img, inv_img))
    local_txt = weight_grad(text_feats, tangent(d_txt, e_txt, inv_txt))
    grad_img, grad_txt, total = lax.psum((local_img, local_txt, local_term), ("img", "txt"))
    batch_total = image_feats.shape[0] * lax.axis_size("img") * lax.axis_size("txt")
    loss = total / (2.0 * batch_total)
    return (loss, grad_img, grad_txt)


MESH = pl.DeviceIdType.MESH
FUSED_VMEM_BYTES = 44 * 1024 * 1024


def dot_nt(a, b):
    return lax.dot_general(a, b, (((1,), (1,)), ((), ())), preferred_element_type=jnp.float32)


def dot_tn(a, b):
    return lax.dot_general(a, b, (((0,), (0,)), ((), ())), preferred_element_type=jnp.float32)


def gather_kernel(n_img, n_txt, image, text, t_img, t_txt, buf, sz, rz, sx, rx, sy, ry, sc, rc, sd, rd, scd, rcd):
    img, txt = lax.axis_index("img"), lax.axis_index("txt")
    nz = n_img // 2
    core = lax.rem(img, 2)
    other = img + 1 - 2 * core
    x_txt = txt + 1 - 2 * lax.rem(txt, 2)
    y_txt = lax.rem(txt + 2, 4)
    d_txt = lax.rem(x_txt + 2, 4)

    def source(k):
        return lax.rem(img + n_img - 2 * k, n_img)

    def slot(i, t):
        return t * n_img + i

    z_peers = [(lax.rem(img + 2 * k, n_img), txt) for k in range(1, nz)]
    peers = z_peers + [(img, x_txt), (img, y_txt), (other, txt)]
    barrier = pltpu.get_barrier_semaphore()
    for peer in peers:
        pl.semaphore_signal(barrier, inc=1, device_id=peer, device_id_type=MESH)

    ft, fi, dt = text.shape[1], image.shape[1], t_img.shape[1]
    half = buf.shape[3]
    split = half - dt - ft
    mine = slot(img, txt)
    buf[mine, 0, :, 0:dt] = t_img[...]
    buf[mine, 0, :, dt : dt + ft] = text[...]
    buf[mine, 0, :, dt + ft : half] = image[:, 0:split]
    buf[mine, 1, :, 0:dt] = t_txt[...]
    buf[mine, 1, :, dt:half] = image[:, split:fi]
    pl.semaphore_wait(barrier, len(peers))

    started = []

    def send(at, part, peer, ssem, rsem):
        ref = buf.at[at] if part is None else buf.at[at, part]
        copy = pltpu.make_async_remote_copy(
            src_ref=ref, dst_ref=ref, send_sem=ssem, recv_sem=rsem, device_id=peer, device_id_type=MESH
        )
        copy.start()
        started.append(copy)

    def arrived(at, part, ssem, rsem):
        ref = buf.at[at] if part is None else buf.at[at, part]
        pltpu.make_async_remote_copy(
            src_ref=ref, dst_ref=ref, send_sem=ssem, recv_sem=rsem, device_id=(other, txt), device_id_type=MESH
        ).wait_recv()

    def line_block(k):
        at = slot(source(k), txt)
        send(at, None, (img, x_txt), sx.at[k], rx.at[k])
        send(at, None, (img, y_txt), sy.at[k], ry.at[k])
        send(at, None, (other, txt), sc.at[0, k], rc.at[0, k])

    for k in range(1, nz):
        send(mine, None, z_peers[k - 1], sz.at[k - 1], rz.at[k - 1])
    line_block(0)
    for k in range(nz):
        if k + 1 < nz:
            arrived(slot(source(k + 1), txt), None, sz.at[k], rz.at[k])
            line_block(k + 1)
        from_x = slot(source(k), x_txt)
        arrived(from_x, None, sx.at[k], rx.at[k])
        send(from_x, 0, (img, y_txt), sd.at[0, k], rd.at[0, k])
        send(from_x, None, (other, txt), sc.at[1, k], rc.at[1, k])
        from_y = slot(source(k), y_txt)
        arrived(from_y, None, sy.at[k], ry.at[k])
        send(from_y, 1, (img, x_txt), sd.at[1, k], rd.at[1, k])
        send(from_y, None, (other, txt), sc.at[2, k], rc.at[2, k])
    for k in range(nz):
        diagonal = slot(source(k), d_txt)
        for part in range(2):
            arrived(diagonal, part, sd.at[part, k], rd.at[part, k])
            send(diagonal, part, (other, txt), scd.at[part, k], rcd.at[part, k])

    other_source = lambda k: lax.rem(other + n_img - 2 * k, n_img)
    for k in range(nz):
        arrived(slot(other_source(k), txt), None, sc.at[0, k], rc.at[0, k])
        arrived(slot(other_source(k), x_txt), None, sc.at[1, k], rc.at[1, k])
        arrived(slot(other_source(k), y_txt), None, sc.at[2, k], rc.at[2, k])
        for part in range(2):
            arrived(slot(other_source(k), d_txt), part, scd.at[part, k], rcd.at[part, k])
    for copy in started:
        copy.wait_send()


def gather_all(n_img, n_txt, image, text, t_img, t_txt):
    rows = image.shape[0]
    half = (image.shape[1] + text.shape[1] + 2 * t_img.shape[1]) // 2
    nz = n_img // 2
    dma = pltpu.SemaphoreType.DMA
    vmem = pl.BlockSpec(memory_space=pltpu.VMEM)
    pairs = [(nz - 1,), (nz,), (nz,), (3, nz), (2, nz), (2, nz)]
    return pl.pallas_call(
        functools.partial(gather_kernel, n_img, n_txt),
        out_shape=jax.ShapeDtypeStruct((n_img * n_txt, 2, rows, half), image.dtype),
        in_specs=[vmem] * 4,
        out_specs=vmem,
        scratch_shapes=[dma(shape) for shape in pairs for _ in range(2)],
        compiler_params=pltpu.CompilerParams(
            collective_id=0, has_side_effects=True, vmem_limit_bytes=FUSED_VMEM_BYTES
        ),
        name="gather_blocks",
    )(image, text, t_img, t_txt)


def loss_kernel(
    buf, w_img, w_txt, loss, grad_img, grad_txt, f_img, e_img, e_txt, s_img, s_txt, q_img, q_txt, i_img, i_txt, tl, sl, ec_t, ec_s, g
):
    slots, _, rows, half = buf.shape
    batch = slots * rows
    fi, ds = w_img.shape
    ft = w_txt.shape[0]
    dt = q_img.shape[1]
    chunk = 128
    per = chunk // rows
    steps = batch // chunk

    def read(c, part, lo, hi):
        return buf[pl.ds(c * per, per), part, :, lo:hi].reshape(chunk, hi - lo)

    def embed(c, _):
        at = pl.ds(pl.multiple_of(c * chunk, chunk), chunk)
        q_img[at, :] = normed(read(c, 0, 0, dt))
        q_txt[at, :] = normed(read(c, 1, 0, dt))
        feats = jnp.concatenate([read(c, 0, dt + ft, half), read(c, 1, dt, half)], axis=1)
        f_img[at, :] = feats
        e, inv = project(feats, w_img[...])
        e_img[at, :], i_img[at, :] = e, inv
        s_img[at, :] = e.astype(jnp.bfloat16)
        e, inv = project(read(c, 0, dt, dt + ft), w_txt[...])
        e_txt[at, :], i_txt[at, :] = e, inv
        s_txt[at, :] = e.astype(jnp.bfloat16)
        return 0

    lax.fori_loop(0, steps, embed, 0)

    def logits(c, maxima):
        at = pl.ds(pl.multiple_of(c * chunk, chunk), chunk)
        t = TEACHER_SCALE * dot_nt(q_img[at, :], q_txt[...])
        s = STUDENT_SCALE * dot_nt(s_img[at, :], s_txt[...])
        tl[at, :], sl[at, :] = t, s
        return (
            jnp.maximum(maxima[0], jnp.max(t, axis=0, keepdims=True)),
            jnp.maximum(maxima[1], jnp.max(s, axis=0, keepdims=True)),
        )

    low = jnp.full((1, batch), -jnp.inf, jnp.float32)
    ctm, csm = lax.fori_loop(0, steps, logits, (low, low))

    def row_terms(c, carry):
        cts, css, terms, lse = carry
        at = pl.ds(pl.multiple_of(c * chunk, chunk), chunk)
        t, s = tl[at, :], sl[at, :]
        rtm, rsm = jnp.max(t, axis=1, keepdims=True), jnp.max(s, axis=1, keepdims=True)
        et, es = jnp.exp(t - rtm), jnp.exp(s - rsm)
        rts, rss = jnp.sum(et, axis=1, keepdims=True), jnp.sum(es, axis=1, keepdims=True)
        p = et * (1.0 / rts)
        diff = t - s
        ct, cs = jnp.exp(t - ctm), jnp.exp(s - csm)
        ec_t[at, :], ec_s[at, :] = ct, cs
        tl[at, :], sl[at, :] = diff, es * (1.0 / rss) - p
        lse = lse + jnp.sum(rsm - rtm + jnp.log(rss) - jnp.log(rts), axis=0, keepdims=True)
        terms = terms + jnp.sum(p * diff, axis=0, keepdims=True)
        return (cts + jnp.sum(ct, axis=0, keepdims=True), css + jnp.sum(cs, axis=0, keepdims=True), terms, lse)

    zero = jnp.zeros((1, batch), jnp.float32)
    cts, css, terms, lse = lax.fori_loop(0, steps, row_terms, (zero, zero, zero, jnp.zeros((1, 1), jnp.float32)))
    rct, rcs = 1.0 / cts, 1.0 / css
    terms = terms + (csm - ctm + jnp.log(css) - jnp.log(cts))

    def columns(c, terms):
        at = pl.ds(pl.multiple_of(c * chunk, chunk), chunk)
        p = ec_t[at, :] * rct
        tile = 0.5 * STUDENT_SCALE * (sl[at, :] + (ec_s[at, :] * rcs - p))
        g[at, :] = tile.astype(jnp.bfloat16)
        return terms + jnp.sum(p * tl[at, :], axis=0, keepdims=True)

    terms = lax.fori_loop(0, steps, columns, terms)
    loss[...] = (jnp.sum(terms, axis=1, keepdims=True) + lse) / (2.0 * batch)

    d_img = jnp.dot(g[...], s_txt[...], preferred_element_type=jnp.float32)
    du = tangent(d_img, e_img[...], i_img[...]).astype(jnp.bfloat16)
    grad_img[...] = dot_tn(f_img[...], du)
    d_txt = dot_tn(g[...], s_img[...])
    du = tangent(d_txt, e_txt[...], i_txt[...]).astype(jnp.bfloat16)
    grad_txt[...] = dot_tn(buf[:, 0, :, dt : dt + ft].reshape(batch, ft), du)


def loss_and_grads(gathered, w_img, w_txt, dt):
    slots, _, rows, half = gathered.shape
    batch = slots * rows
    (fi, ds), ft = w_img.shape, w_txt.shape[0]
    vmem = pl.BlockSpec(memory_space=pltpu.VMEM)
    f32, b16 = jnp.float32, jnp.bfloat16
    scratch = [
        ((batch, fi), b16),
        ((batch, ds), f32),
        ((batch, ds), f32),
        ((batch, ds), b16),
        ((batch, ds), b16),
        ((batch, dt), b16),
        ((batch, dt), b16),
        ((batch, 1), f32),
        ((batch, 1), f32),
    ]
    scratch += [((batch, batch), f32)] * 4 + [((batch, batch), b16)]
    return pl.pallas_call(
        loss_kernel,
        out_shape=[
            jax.ShapeDtypeStruct((1, 1), f32),
            jax.ShapeDtypeStruct((fi, ds), f32),
            jax.ShapeDtypeStruct((ft, ds), f32),
        ],
        in_specs=[vmem] * 3,
        out_specs=[vmem] * 3,
        scratch_shapes=[pltpu.VMEM(*s) for s in scratch],
        compiler_params=pltpu.CompilerParams(vmem_limit_bytes=FUSED_VMEM_BYTES),
        name="loss_and_grads",
    )(gathered, w_img, w_txt)


def whole_batch(n_img, n_txt, image_feats, text_feats, teacher_img, teacher_txt, proj_img, proj_txt):
    gathered = gather_all(n_img, n_txt, image_feats, text_feats, teacher_img, teacher_txt)
    loss, grad_img, grad_txt = loss_and_grads(gathered, proj_img, proj_txt, teacher_img.shape[1])
    return (loss.reshape(()), grad_img, grad_txt)


def fits(n_img, n_txt, image, text, t_img, t_txt, proj_img, proj_txt):
    rows, fi = image.shape
    batch = rows * n_img * n_txt
    ft, dt, ds = text.shape[1], t_img.shape[1], proj_img.shape[1]
    columns = fi + ft + 2 * dt
    split = columns // 2 - dt - ft
    held = 2 * batch * (2 * columns + fi) + 12 * batch * ds + 18 * batch * batch + 6 * ds * (fi + ft)
    aligned = rows % 16 == 0 and 128 % rows == 0 and batch % 128 == 0 and split > 0 and split % 128 == 0 and columns % 256 == 0
    return n_txt == 4 and n_img % 2 == 0 and n_img > 2 and aligned and held <= FUSED_VMEM_BYTES * 3 // 4


def solution(mesh):
    n_img, n_txt = mesh.shape["img"], mesh.shape["txt"]

    def per_device(*arrays):
        if fits(n_img, n_txt, *arrays):
            return whole_batch(n_img, n_txt, *arrays)
        return shards(*arrays)

    return jax.shard_map(
        per_device,
        mesh=mesh,
        in_specs=(
            P(("img", "txt"), None),
            P(("txt", "img"), None),
            P(("img", "txt"), None),
            P(("txt", "img"), None),
            P(),
            P(),
        ),
        out_specs=(P(), P(), P()),
        check_vma=False,
    )
```

```python
import functools

import jax
import jax.numpy as jnp
from jax import lax
from jax.experimental import pallas as pl
from jax.experimental.pallas import tpu as pltpu
from jax.sharding import PartitionSpec as P

EPS = 1e-06
TEACHER_SCALE = 100.0
STUDENT_SCALE = 50.0


def project(feats, weight):
    u = jnp.dot(feats, weight, preferred_element_type=jnp.float32)
    inv = lax.rsqrt(jnp.sum(u * u, axis=1, keepdims=True) + EPS)
    return (u * inv, inv)


def normed(raw):
    x = raw.astype(jnp.float32)
    return (x * lax.rsqrt(jnp.sum(x * x, axis=1, keepdims=True) + EPS)).astype(jnp.bfloat16)


def tangent(grad_rows, embeds, inverse):
    return (grad_rows - embeds * jnp.sum(embeds * grad_rows, 1, keepdims=True)) * inverse


def weight_grad(feats, du_rows):
    return lax.dot_general(
        feats.astype(jnp.float32),
        du_rows,
        (((0,), (0,)), ((), ())),
        precision=lax.Precision.HIGHEST,
    )


def tile_terms(block_q_img, block_q_txt, block_s_img, block_s_txt):
    tl = TEACHER_SCALE * jnp.dot(block_q_img, block_q_txt.T, preferred_element_type=jnp.float32)
    sl = STUDENT_SCALE * jnp.dot(block_s_img, block_s_txt.T, preferred_element_type=jnp.float32)
    rtm, rsm = lax.pmax((tl.max(1), sl.max(1)), "txt")
    rts, rss = lax.psum(
        (jnp.sum(jnp.exp(tl - rtm[:, None]), 1), jnp.sum(jnp.exp(sl - rsm[:, None]), 1)), "txt"
    )
    ctm, csm = lax.pmax((tl.max(0), sl.max(0)), "img")
    cts, css = lax.psum(
        (jnp.sum(jnp.exp(tl - ctm[None, :]), 0), jnp.sum(jnp.exp(sl - csm[None, :]), 0)), "img"
    )
    pt_row = jnp.exp(tl - rtm[:, None]) / rts[:, None]
    ps_row = jnp.exp(sl - rsm[:, None]) / rss[:, None]
    pt_col = jnp.exp(tl - ctm[None, :]) / cts[None, :]
    ps_col = jnp.exp(sl - csm[None, :]) / css[None, :]
    diff = tl - sl
    n_img = lax.axis_size("img")
    n_txt = lax.axis_size("txt")
    local_term = jnp.sum(pt_row * diff) + jnp.sum(pt_col * diff)
    local_term = local_term + jnp.sum(rsm + jnp.log(rss) - rtm - jnp.log(rts)) / n_txt
    local_term = local_term + jnp.sum(csm + jnp.log(css) - ctm - jnp.log(cts)) / n_img
    grad_tile = (0.5 * STUDENT_SCALE * (ps_row - pt_row + (ps_col - pt_col))).astype(jnp.bfloat16)
    part_img = jnp.dot(grad_tile, block_s_txt, preferred_element_type=jnp.float32)
    part_txt = lax.dot_general(
        grad_tile, block_s_img, (((0,), (0,)), ((), ())), preferred_element_type=jnp.float32
    )
    return (part_img, part_txt, local_term)


def shards(image_feats, text_feats, teacher_img, teacher_txt, proj_img, proj_txt):
    e_img, inv_img = project(image_feats, proj_img)
    e_txt, inv_txt = project(text_feats, proj_txt)
    q_img = normed(teacher_img)
    q_txt = normed(teacher_txt)
    feats_img, block_q_img = (
        lax.all_gather(image_feats, "txt", axis=0, tiled=True),
        lax.all_gather(q_img, "txt", axis=0, tiled=True),
    )
    feats_txt, block_q_txt = (
        lax.all_gather(text_feats, "img", axis=0, tiled=True),
        lax.all_gather(q_txt, "img", axis=0, tiled=True),
    )
    block_s_img = project(feats_img, proj_img)[0].astype(jnp.bfloat16)
    block_s_txt = project(feats_txt, proj_txt)[0].astype(jnp.bfloat16)
    part_img, part_txt, local_term = tile_terms(block_q_img, block_q_txt, block_s_img, block_s_txt)
    d_img = lax.psum_scatter(part_img, "txt", scatter_dimension=0, tiled=True)
    d_txt = lax.psum_scatter(part_txt, "img", scatter_dimension=0, tiled=True)
    local_img = weight_grad(image_feats, tangent(d_img, e_img, inv_img))
    local_txt = weight_grad(text_feats, tangent(d_txt, e_txt, inv_txt))
    grad_img, grad_txt, total = lax.psum((local_img, local_txt, local_term), ("img", "txt"))
    batch_total = image_feats.shape[0] * lax.axis_size("img") * lax.axis_size("txt")
    loss = total / (2.0 * batch_total)
    return (loss, grad_img, grad_txt)


MESH = pl.DeviceIdType.MESH
FUSED_VMEM_BYTES = 60 * 1024 * 1024
LANES = 128


def dot_nt(a, b):
    return lax.dot_general(a, b, (((1,), (1,)), ((), ())), preferred_element_type=jnp.float32)


def dot_tn(a, b):
    return lax.dot_general(a, b, (((0,), (0,)), ((), ())), preferred_element_type=jnp.float32)


class Spread:
    def __init__(self, place, buf, halves, sems, log):
        self.place, self.buf, self.halves, self.log = place, buf, halves, log
        self.sz, self.rz, self.sx, self.rx, self.sy, self.ry, self.sc, self.rc, self.sd, self.rd, self.se, self.re = sems

    def ref(self, at, part):
        if part is None:
            return self.buf.at[at]
        lo, hi = self.halves[part]
        return self.buf.at[at, lo:hi]

    def copy(self, at, part, peer, ssem, rsem):
        ref = self.ref(at, part)
        return pltpu.make_async_remote_copy(
            src_ref=ref, dst_ref=ref, send_sem=ssem, recv_sem=rsem, device_id=peer, device_id_type=MESH
        )

    def send(self, *args):
        copy = self.copy(*args)
        copy.start()
        self.log.append(copy)

    def arrived(self, at, part, ssem, rsem):
        self.copy(at, part, self.place.partner, ssem, rsem).wait_recv()

    def own(self):
        p = self.place
        for k in range(1, p.nz):
            self.send(p.slot(p.img, p.txt), None, p.z_peer(k), self.sz.at[k - 1], self.rz.at[k - 1])
        self.line(0)

    def line(self, k):
        p = self.place
        at = p.slot(p.source(k), p.txt)
        if k > 0:
            self.arrived(at, None, self.sz.at[k - 1], self.rz.at[k - 1])
        self.send(at, None, (p.img, p.x_txt), self.sx.at[k], self.rx.at[k])
        self.send(at, None, (p.img, p.y_txt), self.sy.at[k], self.ry.at[k])
        self.send(at, None, p.partner, self.sc.at[0, k], self.rc.at[0, k])

    def turn(self, k):
        p = self.place
        at = p.slot(p.source(k), p.x_txt)
        self.arrived(at, None, self.sx.at[k], self.rx.at[k])
        self.send(at, 0, (p.img, p.y_txt), self.sd.at[0, k], self.rd.at[0, k])
        self.send(at, None, p.partner, self.sc.at[1, k], self.rc.at[1, k])
        at = p.slot(p.source(k), p.y_txt)
        self.arrived(at, None, self.sy.at[k], self.ry.at[k])
        self.send(at, 1, (p.img, p.x_txt), self.sd.at[1, k], self.rd.at[1, k])
        self.send(at, None, p.partner, self.sc.at[2, k], self.rc.at[2, k])

    def last(self, k):
        p = self.place
        at = p.slot(p.source(k), p.d_txt)
        for part in range(2):
            self.arrived(at, part, self.sd.at[part, k], self.rd.at[part, k])
            self.send(at, part, p.partner, self.se.at[part, k], self.re.at[part, k])

    def whole(self, which):
        p = self.place
        for k in range(p.nz):
            source = p.other_source(k)
            if which < 3:
                at = p.slot(source, (p.txt, p.x_txt, p.y_txt)[which])
                self.arrived(at, None, self.sc.at[which, k], self.rc.at[which, k])
            else:
                for part in range(2):
                    self.arrived(p.slot(source, p.d_txt), part, self.se.at[part, k], self.re.at[part, k])


class Place:
    def __init__(self, n_img, n_txt):
        self.n_img, self.n_txt, self.nz = n_img, n_txt, n_img // 2
        self.img, self.txt = lax.axis_index("img"), lax.axis_index("txt")
        self.other = self.img + 1 - 2 * lax.rem(self.img, 2)
        self.partner = (self.other, self.txt)
        self.x_txt = self.txt + 1 - 2 * lax.rem(self.txt, 2)
        self.y_txt = lax.rem(self.txt + 2, 4)
        self.d_txt = lax.rem(self.x_txt + 2, 4)

    def slot(self, img, txt):
        return txt * self.n_img + img

    def source(self, k):
        return lax.rem(self.img + self.n_img - 2 * k, self.n_img)

    def other_source(self, k):
        return lax.rem(self.other + self.n_img - 2 * k, self.n_img)

    def z_peer(self, k):
        return (lax.rem(self.img + 2 * k, self.n_img), self.txt)

    def img_at(self, k):
        return lax.rem(self.img + k, self.n_img)

    def txt_at(self, k):
        return lax.rem(self.txt + k, self.n_txt)


def exchange_kernel(n_img, n_txt, image, text, t_img, t_txt, p_img, p_txt, *refs):
    loss, feats_out, du_img_out, du_txt_out = refs[:4]
    feats, tiles, e_img, e_txt, i_img, i_txt, s_img, s_txt, sl, ps, du_img, du_txt = refs[4:16]
    raw, q_img, q_txt, tile, row_st, col_st, w_img, w_txt, g_tile, load = refs[16:26]
    tz_s, tz_r, tc_s, tc_r, ti_s, ti_r, rs_s, rs_r, cs_s, cs_r = refs[26:36]
    f_sems, p_sems = refs[36:48], refs[48:60]
    p = Place(n_img, n_txt)
    nz, img, txt = p.nz, p.img, p.txt
    rows, fi = image.shape
    ft, dt = text.shape[1], t_img.shape[1]
    half = feats.shape[3]
    batch = sl.shape[0]
    mine = p.slot(img, txt)

    loads = [
        pltpu.make_async_copy(t_img, raw.at[0], load.at[0]),
        pltpu.make_async_copy(t_txt, raw.at[1], load.at[1]),
        pltpu.make_async_copy(image.at[:, 0:half], feats.at[mine, 0], load.at[2]),
        pltpu.make_async_copy(image.at[:, half:fi], feats.at[mine, 1, :, 0 : fi - half], load.at[3]),
        pltpu.make_async_copy(text, feats.at[mine, 1, :, fi - half : half], load.at[4]),
        pltpu.make_async_copy(p_img, w_img, load.at[5]),
        pltpu.make_async_copy(p_txt, w_txt, load.at[6]),
    ]
    for copy in loads:
        copy.start()
    peers = [(p.img_at(k), txt) for k in range(1, n_img)] + [(img, p.txt_at(k)) for k in range(1, n_txt)]
    barrier = pltpu.get_barrier_semaphore()
    for peer in peers:
        pl.semaphore_signal(barrier, inc=1, device_id=peer, device_id_type=MESH)
    loads[0].wait()
    q_img[txt] = normed(raw[0])
    loads[1].wait()
    q_txt[img] = normed(raw[1])
    for copy in loads[2:5]:
        copy.wait()
    pl.semaphore_wait(barrier, len(peers))

    log = []

    def copy_of(ref, peer, ssem, rsem):
        return pltpu.make_async_remote_copy(
            src_ref=ref, dst_ref=ref, send_sem=ssem, recv_sem=rsem, device_id=peer, device_id_type=MESH
        )

    def send(*args):
        copy = copy_of(*args)
        copy.start()
        log.append(copy)

    def arrived(ref, ssem, rsem):
        copy_of(ref, p.partner, ssem, rsem).wait_recv()

    f = Spread(p, feats, ((0, 1), (1, 2)), f_sems, log)
    rows_in, cols_in = rows * n_txt, rows * n_img
    g = Spread(p, tiles, ((0, rows_in // 2), (rows_in // 2, rows_in + 16)), p_sems, log)

    for k in range(1, nz):
        send(q_txt.at[img], p.z_peer(k), tz_s.at[k - 1], tz_r.at[k - 1])
    for k in range(1, n_txt):
        send(q_img.at[txt], (img, p.txt_at(k)), ti_s.at[k - 1], ti_r.at[k - 1])
    send(q_txt.at[img], p.partner, tc_s.at[0], tc_r.at[0])
    f.own()
    for k in range(1, nz):
        arrived(q_txt.at[p.source(k)], tz_s.at[k - 1], tz_r.at[k - 1])
        send(q_txt.at[p.source(k)], p.partner, tc_s.at[k], tc_r.at[k])
    for k in range(1, n_txt):
        arrived(q_img.at[p.txt_at(n_txt - k)], ti_s.at[k - 1], ti_r.at[k - 1])
    for k in range(nz):
        arrived(q_txt.at[p.other_source(k)], tc_s.at[k], tc_r.at[k])

    t = TEACHER_SCALE * dot_nt(q_img[...].reshape(rows_in, dt), q_txt[...].reshape(cols_in, dt))
    tile[...] = t
    m = jnp.max(t, axis=1, keepdims=True)
    s = jnp.sum(jnp.exp(t - m), axis=1, keepdims=True)
    lane = lax.broadcasted_iota(jnp.int32, (rows_in, cols_in), 1)
    packed = jnp.where(lane < rows_in, m, s).T
    row_st[txt] = jnp.zeros(row_st.shape[1:], jnp.float32)
    row_st[txt, 0:1, 0:rows_in] = packed[0:1, :]
    row_st[txt, 1:2, 0:rows_in] = packed[rows_in : rows_in + 1, :]
    m = jnp.max(t, axis=0, keepdims=True)
    col_st[img] = jnp.zeros(col_st.shape[1:], jnp.float32)
    col_st[img, 0:1, :] = m
    col_st[img, 1:2, :] = jnp.sum(jnp.exp(t - m), axis=0, keepdims=True)
    for k in range(1, n_img):
        send(col_st.at[img], (p.img_at(k), txt), cs_s.at[k - 1], cs_r.at[k - 1])
    for k in range(1, n_txt):
        send(row_st.at[txt], (img, p.txt_at(k)), rs_s.at[k - 1], rs_r.at[k - 1])

    for k in range(1, nz):
        f.line(k)
    for k in range(1, n_img):
        arrived(col_st.at[p.img_at(n_img - k)], cs_s.at[k - 1], cs_r.at[k - 1])
    for k in range(1, n_txt):
        arrived(row_st.at[p.txt_at(n_txt - k)], rs_s.at[k - 1], rs_r.at[k - 1])

    def log_sum(stats):
        m = jnp.max(stats[:, 0, :], axis=0, keepdims=True)
        return m + jnp.log(jnp.sum(stats[:, 1, :] * jnp.exp(stats[:, 0, :] - m), axis=0, keepdims=True))

    lz_row = log_sum(row_st[:, :, 0:rows_in])
    lz_col = log_sum(col_st[...])
    t = tile[...]
    both = jnp.exp(t - jnp.broadcast_to(lz_row, (cols_in, rows_in)).T) + jnp.exp(t - lz_col)
    part = jnp.sum(both * t, axis=0, keepdims=True) - lz_col / n_img
    part = part - jnp.sum(lz_row, axis=1, keepdims=True) / (n_txt * cols_in)
    high = part.astype(jnp.bfloat16).astype(jnp.float32)
    middle = (part - high).astype(jnp.bfloat16).astype(jnp.float32)
    line = lax.broadcasted_iota(jnp.int32, (16, cols_in), 0)
    pieces = jnp.where(line == 0, high, jnp.where(line == 1, middle, jnp.where(line == 2, part - high - middle, 0.0)))
    tiles[mine, 0:rows_in, :] = both.astype(jnp.bfloat16)
    tiles[mine, rows_in : rows_in + 16, :] = pieces.astype(jnp.bfloat16)
    g.own()

    def embed(j):
        at = pl.ds(pl.multiple_of(j * cols_in, cols_in), cols_in)
        here = pl.ds(j * n_img, n_img)
        rest = feats[here, 1].reshape(cols_in, half)
        x = jnp.concatenate([feats[here, 0].reshape(cols_in, half), rest[:, 0 : fi - half]], axis=1)
        e, inv = project(x, w_img[...])
        e_img[at, :], i_img[at, :] = e, inv
        s_img[at, :] = e.astype(jnp.bfloat16)
        e, inv = project(rest[:, fi - half : half], w_txt[...])
        e_txt[at, :], i_txt[at, :] = e, inv
        s_txt[at, :] = e.astype(jnp.bfloat16)

    for k in range(nz):
        f.turn(k)
    f.whole(0)
    for copy in loads[5:]:
        copy.wait()
    embed(txt)
    for k in range(1, nz):
        g.line(k)
    for k in range(nz):
        f.last(k)
    f.whole(1)
    embed(p.x_txt)
    for k in range(nz):
        g.turn(k)
    f.whole(2)
    embed(p.y_txt)
    f.whole(3)
    embed(p.d_txt)
    outs = [pltpu.make_async_copy(feats, feats_out, load.at[0])]
    outs[0].start()
    for k in range(nz):
        g.last(k)

    def logits(c, carry):
        csm, total = carry
        at = pl.ds(pl.multiple_of(c * cols_in, cols_in), cols_in)
        s = STUDENT_SCALE * dot_nt(s_img[at, :], s_txt[...])
        sl[at, :] = s
        m = jnp.max(s, axis=1, keepdims=True)
        es = jnp.exp(s - m)
        sums = jnp.sum(es, axis=1, keepdims=True)
        ps[at, :] = es * (1.0 / sums)
        total = total + jnp.sum(m + jnp.log(sums), axis=0, keepdims=True)
        return jnp.maximum(csm, jnp.max(s, axis=0, keepdims=True)), total

    low = jnp.full((1, batch), -jnp.inf, jnp.float32)
    csm, total = lax.fori_loop(0, n_txt, logits, (low, jnp.zeros((1, 1), jnp.float32)))

    def sums(c, css):
        at = pl.ds(pl.multiple_of(c * cols_in, cols_in), cols_in)
        return css + jnp.sum(jnp.exp(sl[at, :] - csm), axis=0, keepdims=True)

    css = lax.fori_loop(0, n_txt, sums, jnp.zeros((1, batch), jnp.float32))
    lzc = csm + jnp.log(css)
    total = total + jnp.sum(lzc, axis=1, keepdims=True)
    for which in range(4):
        g.whole(which)

    def tile_rows(c):
        held = [tiles[i * n_img : (i + 1) * n_img, pl.ds(pl.multiple_of(c * rows, rows), rows), :] for i in range(n_txt)]
        return jnp.concatenate([h.reshape(cols_in, cols_in) for h in held], axis=1).astype(jnp.float32)

    def gradient(c, terms):
        at = pl.ds(pl.multiple_of(c * cols_in, cols_in), cols_in)
        pt, s = tile_rows(c), sl[at, :]
        g_tile[at, :] = (0.5 * STUDENT_SCALE * (ps[at, :] + jnp.exp(s - lzc) - pt)).astype(jnp.bfloat16)
        return terms - jnp.sum(pt * s, axis=0, keepdims=True)

    terms = lax.fori_loop(0, n_txt, gradient, jnp.zeros((1, batch), jnp.float32))
    d_img = jnp.dot(g_tile[...], s_txt[...], preferred_element_type=jnp.float32)
    du_img[...] = tangent(d_img, e_img[...], i_img[...]).astype(jnp.bfloat16)
    outs.append(pltpu.make_async_copy(du_img, du_img_out, load.at[1]))
    outs[1].start()
    d_txt = dot_tn(g_tile[...], s_img[...])
    du_txt[...] = tangent(d_txt, e_txt[...], i_txt[...]).astype(jnp.bfloat16)
    outs.append(pltpu.make_async_copy(du_txt, du_txt_out, load.at[2]))
    outs[2].start()
    parts = jnp.sum(tiles[:, rows_in : rows_in + 16, :].astype(jnp.float32), axis=0)
    total = total + jnp.sum(terms, axis=1, keepdims=True)
    total = total + jnp.sum(jnp.sum(parts, axis=0, keepdims=True), axis=1, keepdims=True)
    loss[...] = total / (2.0 * batch)
    for copy in log:
        copy.wait_send()
    for copy in outs:
        copy.wait()


def exchange(n_img, n_txt, image, text, t_img, t_txt, w_img, w_txt):
    rows, fi = image.shape
    ft, dt, ds = text.shape[1], t_img.shape[1], w_img.shape[1]
    nz, slots = n_img // 2, n_img * n_txt
    batch, rows_in, cols_in = rows * slots, rows * n_txt, rows * n_img
    f32, b16 = jnp.float32, jnp.bfloat16
    dma = pltpu.SemaphoreType.DMA
    vmem = pl.BlockSpec(memory_space=pltpu.VMEM)
    hbm = pl.BlockSpec(memory_space=pltpu.HBM)
    outs = [((1, 1), f32), ((slots, 2, rows, (fi + ft) // 2), b16), ((batch, ds), b16), ((batch, ds), b16)]
    held = [
        ((slots, 2, rows, (fi + ft) // 2), b16),
        ((slots, rows_in + 16, cols_in), b16),
        ((batch, ds), f32),
        ((batch, ds), f32),
        ((batch, 1), f32),
        ((batch, 1), f32),
        ((batch, ds), b16),
        ((batch, ds), b16),
        ((batch, batch), f32),
        ((batch, batch), f32),
        ((batch, ds), b16),
        ((batch, ds), b16),
    ]
    scratch = [pltpu.VMEM(*h) for h in held] + [
        pltpu.VMEM((2, rows, dt), b16),
        pltpu.VMEM((n_txt, rows, dt), b16),
        pltpu.VMEM((n_img, rows, dt), b16),
        pltpu.VMEM((rows_in, cols_in), f32),
        pltpu.VMEM((n_txt, 8, LANES), f32),
        pltpu.VMEM((n_img, 8, LANES), f32),
        pltpu.VMEM((fi, ds), b16),
        pltpu.VMEM((ft, ds), b16),
        pltpu.VMEM((batch, batch), b16),
        dma((7,)),
    ]
    spread = [(nz - 1,), (nz,), (nz,), (3, nz), (2, nz), (2, nz)]
    for shape in [(nz - 1,), (nz,), (n_txt - 1,), (n_txt - 1,), (n_img - 1,)] + spread + spread:
        scratch += [dma(shape), dma(shape)]
    return pl.pallas_call(
        functools.partial(exchange_kernel, n_img, n_txt),
        out_shape=[jax.ShapeDtypeStruct(*s) for s in outs],
        in_specs=[hbm] * 6,
        out_specs=[vmem] + [hbm] * 3,
        scratch_shapes=scratch,
        compiler_params=pltpu.CompilerParams(
            collective_id=0, has_side_effects=True, vmem_limit_bytes=FUSED_VMEM_BYTES
        ),
        name="exchange_and_embed",
    )(image, text, t_img, t_txt, w_img, w_txt)


def grads_kernel(loss_in, feats_in, du_img_in, du_txt_in, loss, grad_img, grad_txt, feats, du_img, du_txt, g_img, g_txt, load, store):
    slots, _, rows, half = feats.shape
    batch = slots * rows
    fi = grad_img.shape[0]
    loads = [
        pltpu.make_async_copy(du_img_in, du_img, load.at[0]),
        pltpu.make_async_copy(feats_in, feats, load.at[1]),
        pltpu.make_async_copy(du_txt_in, du_txt, load.at[2]),
    ]
    for copy in loads:
        copy.start()
    loss[...] = loss_in[...]
    for copy in loads[:2]:
        copy.wait()
    g_img[0:half, :] = dot_tn(feats[:, 0].reshape(batch, half), du_img[...])
    first = pltpu.make_async_copy(g_img.at[0:half], grad_img.at[0:half], store.at[0])
    first.start()
    g_img[half:fi, :] = dot_tn(feats[:, 1, :, 0 : fi - half].reshape(batch, fi - half), du_img[...])
    second = pltpu.make_async_copy(g_img.at[half:fi], grad_img.at[half:fi], store.at[1])
    second.start()
    loads[2].wait()
    g_txt[...] = dot_tn(feats[:, 1, :, fi - half : half].reshape(batch, 2 * half - fi), du_txt[...])
    third = pltpu.make_async_copy(g_txt, grad_txt, store.at[2])
    third.start()
    for copy in (first, second, third):
        copy.wait()


def whole_batch(n_img, n_txt, image_feats, text_feats, teacher_img, teacher_txt, proj_img, proj_txt):
    held = exchange(n_img, n_txt, image_feats, text_feats, teacher_img, teacher_txt, proj_img, proj_txt)
    (fi, ds), ft = proj_img.shape, proj_txt.shape[0]
    vmem = pl.BlockSpec(memory_space=pltpu.VMEM)
    hbm = pl.BlockSpec(memory_space=pltpu.HBM)
    f32 = jnp.float32
    loss, grad_img, grad_txt = pl.pallas_call(
        grads_kernel,
        out_shape=[
            jax.ShapeDtypeStruct((1, 1), f32),
            jax.ShapeDtypeStruct((fi, ds), f32),
            jax.ShapeDtypeStruct((ft, ds), f32),
        ],
        in_specs=[vmem] + [hbm] * 3,
        out_specs=[vmem] + [hbm] * 2,
        scratch_shapes=[pltpu.VMEM(h.shape, h.dtype) for h in held[1:]]
        + [
            pltpu.VMEM((fi, ds), f32),
            pltpu.VMEM((ft, ds), f32),
            pltpu.SemaphoreType.DMA((3,)),
            pltpu.SemaphoreType.DMA((3,)),
        ],
        compiler_params=pltpu.CompilerParams(vmem_limit_bytes=FUSED_VMEM_BYTES),
        name="weight_grads",
    )(*held)
    return (loss.reshape(()), grad_img, grad_txt)


def fits(n_img, n_txt, image, text, t_img, t_txt, proj_img, proj_txt):
    rows, fi = image.shape
    batch = rows * n_img * n_txt
    ft, dt, ds = text.shape[1], t_img.shape[1], proj_img.shape[1]
    half = (fi + ft) // 2
    held = 2 * batch * (fi + ft) + 12 * batch * ds + 16 * batch * batch + 6 * ds * (fi + ft)
    aligned = rows % 16 == 0 and rows * n_img == LANES and rows * n_txt * 2 <= LANES and ft % 128 == 0 and dt % 128 == 0
    aligned = aligned and fi % 128 == 0 and (fi + ft) % 256 == 0 and half < fi and (rows * n_txt) % 32 == 0
    return n_txt == 4 and n_img % 2 == 0 and n_img > 2 and aligned and held <= FUSED_VMEM_BYTES * 3 // 4


def solution(mesh):
    n_img, n_txt = mesh.shape["img"], mesh.shape["txt"]

    def per_device(*arrays):
        if fits(n_img, n_txt, *arrays):
            return whole_batch(n_img, n_txt, *arrays)
        return shards(*arrays)

    return jax.shard_map(
        per_device,
        mesh=mesh,
        in_specs=(
            P(("img", "txt"), None),
            P(("txt", "img"), None),
            P(("img", "txt"), None),
            P(("txt", "img"), None),
            P(),
            P(),
        ),
        out_specs=(P(), P(), P()),
        check_vma=False,
    )
```

```python
import functools

import jax
import jax.numpy as jnp
from jax import lax
from jax.experimental import pallas as pl
from jax.experimental.pallas import tpu as pltpu
from jax.sharding import PartitionSpec as P

EPS = 1e-06
TEACHER_SCALE = 100.0
STUDENT_SCALE = 50.0


def project(feats, weight):
    u = jnp.dot(feats, weight, preferred_element_type=jnp.float32)
    inv = lax.rsqrt(jnp.sum(u * u, axis=1, keepdims=True) + EPS)
    return (u * inv, inv)


def normed(raw):
    x = raw.astype(jnp.float32)
    return (x * lax.rsqrt(jnp.sum(x * x, axis=1, keepdims=True) + EPS)).astype(jnp.bfloat16)


def tangent(grad_rows, embeds, inverse):
    return (grad_rows - embeds * jnp.sum(embeds * grad_rows, 1, keepdims=True)) * inverse


def weight_grad(feats, du_rows):
    return lax.dot_general(
        feats.astype(jnp.float32),
        du_rows,
        (((0,), (0,)), ((), ())),
        precision=lax.Precision.HIGHEST,
    )


def tile_terms(block_q_img, block_q_txt, block_s_img, block_s_txt):
    tl = TEACHER_SCALE * jnp.dot(block_q_img, block_q_txt.T, preferred_element_type=jnp.float32)
    sl = STUDENT_SCALE * jnp.dot(block_s_img, block_s_txt.T, preferred_element_type=jnp.float32)
    rtm, rsm = lax.pmax((tl.max(1), sl.max(1)), "txt")
    rts, rss = lax.psum(
        (jnp.sum(jnp.exp(tl - rtm[:, None]), 1), jnp.sum(jnp.exp(sl - rsm[:, None]), 1)), "txt"
    )
    ctm, csm = lax.pmax((tl.max(0), sl.max(0)), "img")
    cts, css = lax.psum(
        (jnp.sum(jnp.exp(tl - ctm[None, :]), 0), jnp.sum(jnp.exp(sl - csm[None, :]), 0)), "img"
    )
    pt_row = jnp.exp(tl - rtm[:, None]) / rts[:, None]
    ps_row = jnp.exp(sl - rsm[:, None]) / rss[:, None]
    pt_col = jnp.exp(tl - ctm[None, :]) / cts[None, :]
    ps_col = jnp.exp(sl - csm[None, :]) / css[None, :]
    diff = tl - sl
    n_img = lax.axis_size("img")
    n_txt = lax.axis_size("txt")
    local_term = jnp.sum(pt_row * diff) + jnp.sum(pt_col * diff)
    local_term = local_term + jnp.sum(rsm + jnp.log(rss) - rtm - jnp.log(rts)) / n_txt
    local_term = local_term + jnp.sum(csm + jnp.log(css) - ctm - jnp.log(cts)) / n_img
    grad_tile = (0.5 * STUDENT_SCALE * (ps_row - pt_row + (ps_col - pt_col))).astype(jnp.bfloat16)
    part_img = jnp.dot(grad_tile, block_s_txt, preferred_element_type=jnp.float32)
    part_txt = lax.dot_general(
        grad_tile, block_s_img, (((0,), (0,)), ((), ())), preferred_element_type=jnp.float32
    )
    return (part_img, part_txt, local_term)


def shards(image_feats, text_feats, teacher_img, teacher_txt, proj_img, proj_txt):
    e_img, inv_img = project(image_feats, proj_img)
    e_txt, inv_txt = project(text_feats, proj_txt)
    q_img = normed(teacher_img)
    q_txt = normed(teacher_txt)
    feats_img, block_q_img = (
        lax.all_gather(image_feats, "txt", axis=0, tiled=True),
        lax.all_gather(q_img, "txt", axis=0, tiled=True),
    )
    feats_txt, block_q_txt = (
        lax.all_gather(text_feats, "img", axis=0, tiled=True),
        lax.all_gather(q_txt, "img", axis=0, tiled=True),
    )
    block_s_img = project(feats_img, proj_img)[0].astype(jnp.bfloat16)
    block_s_txt = project(feats_txt, proj_txt)[0].astype(jnp.bfloat16)
    part_img, part_txt, local_term = tile_terms(block_q_img, block_q_txt, block_s_img, block_s_txt)
    d_img = lax.psum_scatter(part_img, "txt", scatter_dimension=0, tiled=True)
    d_txt = lax.psum_scatter(part_txt, "img", scatter_dimension=0, tiled=True)
    local_img = weight_grad(image_feats, tangent(d_img, e_img, inv_img))
    local_txt = weight_grad(text_feats, tangent(d_txt, e_txt, inv_txt))
    grad_img, grad_txt, total = lax.psum((local_img, local_txt, local_term), ("img", "txt"))
    batch_total = image_feats.shape[0] * lax.axis_size("img") * lax.axis_size("txt")
    loss = total / (2.0 * batch_total)
    return (loss, grad_img, grad_txt)


MESH = pl.DeviceIdType.MESH
FUSED_VMEM_BYTES = 60 * 1024 * 1024
LANES = 128


def dot_nt(a, b):
    return lax.dot_general(a, b, (((1,), (1,)), ((), ())), preferred_element_type=jnp.float32)


def dot_tn(a, b):
    return lax.dot_general(a, b, (((0,), (0,)), ((), ())), preferred_element_type=jnp.float32)


class Spread:
    def __init__(self, place, buf, halves, sems, log, straight=False):
        self.place, self.buf, self.halves, self.log, self.straight = place, buf, halves, log, straight
        self.sz, self.rz, self.sx, self.rx, self.sy, self.ry, self.sc, self.rc, self.sd, self.rd, self.se, self.re = sems

    def ref(self, at, part):
        if part is None:
            return self.buf.at[at]
        lo, hi = self.halves[part]
        return self.buf.at[at, lo:hi]

    def copy(self, at, part, peer, ssem, rsem):
        ref = self.ref(at, part)
        return pltpu.make_async_remote_copy(
            src_ref=ref, dst_ref=ref, send_sem=ssem, recv_sem=rsem, device_id=peer, device_id_type=MESH
        )

    def send(self, *args):
        copy = self.copy(*args)
        copy.start()
        self.log.append(copy)

    def arrived(self, at, part, ssem, rsem):
        self.copy(at, part, self.place.partner, ssem, rsem).wait_recv()

    def own_z(self):
        p = self.place
        for k in range(1, p.nz):
            self.send(p.slot(p.img, p.txt), None, p.z_peer(k), self.sz.at[k - 1], self.rz.at[k - 1])

    def line(self, k):
        p = self.place
        at = p.slot(p.source(k), p.txt)
        if k > 0:
            self.arrived(at, None, self.sz.at[k - 1], self.rz.at[k - 1])
        self.send(at, None, (p.img, p.x_txt), self.sx.at[k], self.rx.at[k])
        self.send(at, None, (p.img, p.y_txt), self.sy.at[k], self.ry.at[k])
        if self.straight:
            self.send(at, None, (p.img, p.d_txt), self.sd.at[0, k], self.rd.at[0, k])
        self.send(at, None, p.partner, self.sc.at[0, k], self.rc.at[0, k])

    def turn(self, k):
        p = self.place
        at = p.slot(p.source(k), p.x_txt)
        self.arrived(at, None, self.sx.at[k], self.rx.at[k])
        if not self.straight:
            self.send(at, 0, (p.img, p.y_txt), self.sd.at[0, k], self.rd.at[0, k])
        self.send(at, None, p.partner, self.sc.at[1, k], self.rc.at[1, k])
        at = p.slot(p.source(k), p.y_txt)
        self.arrived(at, None, self.sy.at[k], self.ry.at[k])
        if not self.straight:
            self.send(at, 1, (p.img, p.x_txt), self.sd.at[1, k], self.rd.at[1, k])
        self.send(at, None, p.partner, self.sc.at[2, k], self.rc.at[2, k])

    def last(self, k):
        p = self.place
        at = p.slot(p.source(k), p.d_txt)
        for i, part in self.parts():
            self.arrived(at, part, self.sd.at[i, k], self.rd.at[i, k])
            self.send(at, part, p.partner, self.se.at[i, k], self.re.at[i, k])

    def parts(self):
        return ((0, None),) if self.straight else ((0, 0), (1, 1))

    def whole(self, which):
        p = self.place
        for k in range(p.nz):
            source = p.other_source(k)
            if which < 3:
                at = p.slot(source, (p.txt, p.x_txt, p.y_txt)[which])
                self.arrived(at, None, self.sc.at[which, k], self.rc.at[which, k])
            else:
                for i, part in self.parts():
                    self.arrived(p.slot(source, p.d_txt), part, self.se.at[i, k], self.re.at[i, k])


class Place:
    def __init__(self, n_img, n_txt):
        self.n_img, self.n_txt, self.nz = n_img, n_txt, n_img // 2
        self.img, self.txt = lax.axis_index("img"), lax.axis_index("txt")
        self.other = self.img + 1 - 2 * lax.rem(self.img, 2)
        self.partner = (self.other, self.txt)
        self.x_txt = self.txt + 1 - 2 * lax.rem(self.txt, 2)
        self.y_txt = lax.rem(self.txt + 2, 4)
        self.d_txt = lax.rem(self.x_txt + 2, 4)

    def slot(self, img, txt):
        return txt * self.n_img + img

    def source(self, k):
        return lax.rem(self.img + self.n_img - 2 * k, self.n_img)

    def other_source(self, k):
        return lax.rem(self.other + self.n_img - 2 * k, self.n_img)

    def z_peer(self, k):
        return (lax.rem(self.img + 2 * k, self.n_img), self.txt)

    def img_at(self, k):
        return lax.rem(self.img + k, self.n_img)

    def txt_at(self, k):
        return lax.rem(self.txt + k, self.n_txt)


def exchange_kernel(n_img, n_txt, image, text, t_img, t_txt, p_img, p_txt, *refs):
    loss, turned_out, du_img_out, du_txt_out = refs[:4]
    feats, tiles, e_img, e_txt, i_img, i_txt, s_img, s_txt, sl, ps, du_img, du_txt = refs[4:16]
    turned = refs[60]
    raw, q_img, q_txt, tile, row_st, col_st, w_img, w_txt, g_tile, load = refs[16:26]
    tz_s, tz_r, tc_s, tc_r, ti_s, ti_r, rs_s, rs_r, cs_s, cs_r = refs[26:36]
    f_sems, p_sems = refs[36:48], refs[48:60]
    p = Place(n_img, n_txt)
    nz, img, txt = p.nz, p.img, p.txt
    rows, fi = image.shape
    ft, dt = text.shape[1], t_img.shape[1]
    half = feats.shape[3]
    batch = sl.shape[0]
    mine = p.slot(img, txt)

    loads = [
        pltpu.make_async_copy(t_img, raw.at[0], load.at[0]),
        pltpu.make_async_copy(t_txt, raw.at[1], load.at[1]),
        pltpu.make_async_copy(image.at[:, 0:half], feats.at[mine, 0], load.at[2]),
        pltpu.make_async_copy(image.at[:, half:fi], feats.at[mine, 1, :, 0 : fi - half], load.at[3]),
        pltpu.make_async_copy(text, feats.at[mine, 1, :, fi - half : half], load.at[4]),
        pltpu.make_async_copy(p_img, w_img, load.at[5]),
        pltpu.make_async_copy(p_txt, w_txt, load.at[6]),
    ]
    for copy in loads:
        copy.start()
    peers = [(p.img_at(k), txt) for k in range(1, n_img)] + [(img, p.txt_at(k)) for k in range(1, n_txt)]
    barrier = pltpu.get_barrier_semaphore()
    for peer in peers:
        pl.semaphore_signal(barrier, inc=1, device_id=peer, device_id_type=MESH)
    loads[0].wait()
    q_img[txt] = normed(raw[0])
    loads[1].wait()
    q_txt[img] = normed(raw[1])
    for copy in loads[2:5]:
        copy.wait()
    pl.semaphore_wait(barrier, len(peers))

    log = []

    def copy_of(ref, peer, ssem, rsem):
        return pltpu.make_async_remote_copy(
            src_ref=ref, dst_ref=ref, send_sem=ssem, recv_sem=rsem, device_id=peer, device_id_type=MESH
        )

    def send(*args):
        copy = copy_of(*args)
        copy.start()
        log.append(copy)

    def arrived(ref, ssem, rsem):
        copy_of(ref, p.partner, ssem, rsem).wait_recv()

    f = Spread(p, feats, ((0, 1), (1, 2)), f_sems, log)
    rows_in, cols_in = rows * n_txt, rows * n_img
    g = Spread(p, tiles, ((0, rows_in // 2), (rows_in // 2, rows_in + 16)), p_sems, log, straight=True)

    for k in range(1, nz):
        send(q_txt.at[img], p.z_peer(k), tz_s.at[k - 1], tz_r.at[k - 1])
    for k in range(1, n_txt):
        send(q_img.at[txt], (img, p.txt_at(k)), ti_s.at[k - 1], ti_r.at[k - 1])
    send(q_txt.at[img], p.partner, tc_s.at[0], tc_r.at[0])
    f.line(0)
    for copy in log[: nz - 1]:
        copy.wait_send()
    del log[: nz - 1]
    f.own_z()
    for k in range(1, nz):
        arrived(q_txt.at[p.source(k)], tz_s.at[k - 1], tz_r.at[k - 1])
        send(q_txt.at[p.source(k)], p.partner, tc_s.at[k], tc_r.at[k])
    for k in range(1, n_txt):
        arrived(q_img.at[p.txt_at(n_txt - k)], ti_s.at[k - 1], ti_r.at[k - 1])
    for k in range(nz):
        arrived(q_txt.at[p.other_source(k)], tc_s.at[k], tc_r.at[k])

    t = TEACHER_SCALE * dot_nt(q_img[...].reshape(rows_in, dt), q_txt[...].reshape(cols_in, dt))
    tile[...] = t
    m = jnp.max(t, axis=1, keepdims=True)
    s = jnp.sum(jnp.exp(t - m), axis=1, keepdims=True)
    lane = lax.broadcasted_iota(jnp.int32, (rows_in, cols_in), 1)
    packed = jnp.where(lane < rows_in, m, s).T
    row_st[txt] = jnp.zeros(row_st.shape[1:], jnp.float32)
    row_st[txt, 0:1, 0:rows_in] = packed[0:1, :]
    row_st[txt, 1:2, 0:rows_in] = packed[rows_in : rows_in + 1, :]
    m = jnp.max(t, axis=0, keepdims=True)
    col_st[img] = jnp.zeros(col_st.shape[1:], jnp.float32)
    col_st[img, 0:1, :] = m
    col_st[img, 1:2, :] = jnp.sum(jnp.exp(t - m), axis=0, keepdims=True)
    for k in range(1, n_img):
        send(col_st.at[img], (p.img_at(k), txt), cs_s.at[k - 1], cs_r.at[k - 1])
    for k in range(1, n_txt):
        send(row_st.at[txt], (img, p.txt_at(k)), rs_s.at[k - 1], rs_r.at[k - 1])

    for k in range(1, nz):
        f.line(k)
    for k in range(1, n_img):
        arrived(col_st.at[p.img_at(n_img - k)], cs_s.at[k - 1], cs_r.at[k - 1])
    for k in range(1, n_txt):
        arrived(row_st.at[p.txt_at(n_txt - k)], rs_s.at[k - 1], rs_r.at[k - 1])

    def log_sum(stats):
        m = jnp.max(stats[:, 0, :], axis=0, keepdims=True)
        return m + jnp.log(jnp.sum(stats[:, 1, :] * jnp.exp(stats[:, 0, :] - m), axis=0, keepdims=True))

    lz_row = log_sum(row_st[:, :, 0:rows_in])
    lz_col = log_sum(col_st[...])
    t = tile[...]
    both = jnp.exp(t - jnp.broadcast_to(lz_row, (cols_in, rows_in)).T) + jnp.exp(t - lz_col)
    part = jnp.sum(both * t, axis=0, keepdims=True) - lz_col / n_img
    part = part - jnp.sum(lz_row, axis=1, keepdims=True) / (n_txt * cols_in)
    high = part.astype(jnp.bfloat16).astype(jnp.float32)
    middle = (part - high).astype(jnp.bfloat16).astype(jnp.float32)
    line = lax.broadcasted_iota(jnp.int32, (16, cols_in), 0)
    pieces = jnp.where(line == 0, high, jnp.where(line == 1, middle, jnp.where(line == 2, part - high - middle, 0.0)))
    tiles[mine, 0:rows_in, :] = both.astype(jnp.bfloat16)
    tiles[mine, rows_in : rows_in + 16, :] = pieces.astype(jnp.bfloat16)
    g.own_z()
    g.line(0)

    def embed(j):
        at = pl.ds(pl.multiple_of(j * cols_in, cols_in), cols_in)
        here = pl.ds(j * n_img, n_img)
        rest = feats[here, 1].reshape(cols_in, half)
        x = jnp.concatenate([feats[here, 0].reshape(cols_in, half), rest[:, 0 : fi - half]], axis=1)
        turned[0:fi, at] = x.T
        turned[fi : fi + ft, at] = rest[:, fi - half : half].T
        e, inv = project(x, w_img[...])
        e_img[at, :], i_img[at, :] = e, inv
        s_img[at, :] = e.astype(jnp.bfloat16)
        e, inv = project(rest[:, fi - half : half], w_txt[...])
        e_txt[at, :], i_txt[at, :] = e, inv
        s_txt[at, :] = e.astype(jnp.bfloat16)

    for k in range(nz):
        f.turn(k)
    f.whole(0)
    for copy in loads[5:]:
        copy.wait()
    embed(txt)
    for k in range(1, nz):
        g.line(k)
    for k in range(nz):
        f.last(k)
    f.whole(1)
    embed(p.x_txt)
    for k in range(nz):
        g.turn(k)
    f.whole(2)
    embed(p.y_txt)
    f.whole(3)
    embed(p.d_txt)
    outs = [pltpu.make_async_copy(turned, turned_out, load.at[0])]
    outs[0].start()
    for k in range(nz):
        g.last(k)

    chunks = [slice(c * cols_in, (c + 1) * cols_in) for c in range(n_txt)]
    csm = jnp.full((1, batch), -jnp.inf, jnp.float32)
    total = jnp.zeros((1, 1), jnp.float32)
    for at in chunks:
        s = STUDENT_SCALE * dot_nt(s_img[at, :], s_txt[...])
        sl[at, :] = s
        m = jnp.max(s, axis=1, keepdims=True)
        es = jnp.exp(s - m)
        sums = jnp.sum(es, axis=1, keepdims=True)
        ps[at, :] = es * (1.0 / sums)
        total = total + jnp.sum(m + jnp.log(sums), axis=0, keepdims=True)
        csm = jnp.maximum(csm, jnp.max(s, axis=0, keepdims=True))
    css = jnp.zeros((1, batch), jnp.float32)
    for at in chunks:
        css = css + jnp.sum(jnp.exp(sl[at, :] - csm), axis=0, keepdims=True)
    lzc = csm + jnp.log(css)
    total = total + jnp.sum(lzc, axis=1, keepdims=True)
    for at in chunks:
        ps[at, :] = ps[at, :] + jnp.exp(sl[at, :] - lzc)
    for copy in log:
        copy.wait_send()
    for which in range(4):
        g.whole(which)

    def tile_rows(c):
        held = [tiles[i * n_img : (i + 1) * n_img, c * rows : (c + 1) * rows, :] for i in range(n_txt)]
        return jnp.concatenate([h.reshape(cols_in, cols_in) for h in held], axis=1).astype(jnp.float32)

    terms = jnp.zeros((1, batch), jnp.float32)
    for c, at in enumerate(chunks):
        pt = tile_rows(c)
        tile_g = (0.5 * STUDENT_SCALE * (ps[at, :] - pt)).astype(jnp.bfloat16)
        g_tile[at, :] = tile_g
        terms = terms - jnp.sum(pt * sl[at, :], axis=0, keepdims=True)
        d_img = jnp.dot(tile_g, s_txt[...], preferred_element_type=jnp.float32)
        du_img[at, :] = tangent(d_img, e_img[at, :], i_img[at, :]).astype(jnp.bfloat16)
    outs.append(pltpu.make_async_copy(du_img, du_img_out, load.at[1]))
    outs[1].start()
    for at in chunks:
        d_txt = dot_tn(g_tile[:, at], s_img[...])
        du_txt[at, :] = tangent(d_txt, e_txt[at, :], i_txt[at, :]).astype(jnp.bfloat16)
    outs.append(pltpu.make_async_copy(du_txt, du_txt_out, load.at[2]))
    outs[2].start()
    parts = jnp.sum(tiles[:, rows_in : rows_in + 16, :].astype(jnp.float32), axis=0)
    total = total + jnp.sum(terms, axis=1, keepdims=True)
    total = total + jnp.sum(jnp.sum(parts, axis=0, keepdims=True), axis=1, keepdims=True)
    loss[...] = total / (2.0 * batch)
    for copy in outs:
        copy.wait()


def exchange(n_img, n_txt, image, text, t_img, t_txt, w_img, w_txt):
    rows, fi = image.shape
    ft, dt, ds = text.shape[1], t_img.shape[1], w_img.shape[1]
    nz, slots = n_img // 2, n_img * n_txt
    batch, rows_in, cols_in = rows * slots, rows * n_txt, rows * n_img
    f32, b16 = jnp.float32, jnp.bfloat16
    dma = pltpu.SemaphoreType.DMA
    vmem = pl.BlockSpec(memory_space=pltpu.VMEM)
    hbm = pl.BlockSpec(memory_space=pltpu.HBM)
    outs = [((1, 1), f32), ((fi + ft, batch), b16), ((batch, ds), b16), ((batch, ds), b16)]
    held = [
        ((slots, 2, rows, (fi + ft) // 2), b16),
        ((slots, rows_in + 16, cols_in), b16),
        ((batch, ds), f32),
        ((batch, ds), f32),
        ((batch, 1), f32),
        ((batch, 1), f32),
        ((batch, ds), b16),
        ((batch, ds), b16),
        ((batch, batch), f32),
        ((batch, batch), f32),
        ((batch, ds), b16),
        ((batch, ds), b16),
    ]
    scratch = [pltpu.VMEM(*h) for h in held] + [
        pltpu.VMEM((2, rows, dt), b16),
        pltpu.VMEM((n_txt, rows, dt), b16),
        pltpu.VMEM((n_img, rows, dt), b16),
        pltpu.VMEM((rows_in, cols_in), f32),
        pltpu.VMEM((n_txt, 8, LANES), f32),
        pltpu.VMEM((n_img, 8, LANES), f32),
        pltpu.VMEM((fi, ds), b16),
        pltpu.VMEM((ft, ds), b16),
        pltpu.VMEM((batch, batch), b16),
        dma((7,)),
    ]
    spread = [(nz - 1,), (nz,), (nz,), (3, nz), (2, nz), (2, nz)]
    for shape in [(nz - 1,), (nz,), (n_txt - 1,), (n_txt - 1,), (n_img - 1,)] + spread + spread:
        scratch += [dma(shape), dma(shape)]
    scratch.append(pltpu.VMEM((fi + ft, batch), b16))
    return pl.pallas_call(
        functools.partial(exchange_kernel, n_img, n_txt),
        out_shape=[jax.ShapeDtypeStruct(*s) for s in outs],
        in_specs=[hbm] * 6,
        out_specs=[vmem] + [hbm] * 3,
        scratch_shapes=scratch,
        compiler_params=pltpu.CompilerParams(
            collective_id=0, has_side_effects=True, vmem_limit_bytes=FUSED_VMEM_BYTES
        ),
        name="exchange_and_embed",
    )(image, text, t_img, t_txt, w_img, w_txt)


def grads_kernel(loss_in, turned_in, du_img_in, du_txt_in, loss, grad_img, grad_txt, turned, du_img, du_txt, g_img, g_txt, load, store):
    fi, ft = grad_img.shape[0], grad_txt.shape[0]
    step = LANES * 2
    loads = [
        pltpu.make_async_copy(du_img_in, du_img, load.at[0]),
        pltpu.make_async_copy(turned_in.at[0:step], turned.at[0:step], load.at[1]),
        pltpu.make_async_copy(turned_in.at[step : fi + ft], turned.at[step : fi + ft], load.at[2]),
        pltpu.make_async_copy(du_txt_in, du_txt, load.at[3]),
    ]
    for copy in loads:
        copy.start()
    loss[...] = loss_in[...]
    stores = []

    def block(lo, at, du, held, out):
        rows = min(step, held.shape[0] - at)
        here = slice(at, at + rows)
        held[here, :] = jnp.dot(turned[lo + at : lo + at + rows, :], du[...], preferred_element_type=jnp.float32)
        copy = pltpu.make_async_copy(held.at[here], out.at[here], store.at[len(stores)])
        copy.start()
        stores.append(copy)

    for copy in loads[:2]:
        copy.wait()
    for at in range(0, fi, step):
        if at == step:
            loads[2].wait()
        block(0, at, du_img, g_img, grad_img)
    if fi <= step:
        loads[2].wait()
    loads[3].wait()
    for at in range(0, ft, step):
        block(fi, at, du_txt, g_txt, grad_txt)
    for copy in stores:
        copy.wait()


def whole_batch(n_img, n_txt, image_feats, text_feats, teacher_img, teacher_txt, proj_img, proj_txt):
    held = exchange(n_img, n_txt, image_feats, text_feats, teacher_img, teacher_txt, proj_img, proj_txt)
    (fi, ds), ft = proj_img.shape, proj_txt.shape[0]
    vmem = pl.BlockSpec(memory_space=pltpu.VMEM)
    hbm = pl.BlockSpec(memory_space=pltpu.HBM)
    f32 = jnp.float32
    loss, grad_img, grad_txt = pl.pallas_call(
        grads_kernel,
        out_shape=[
            jax.ShapeDtypeStruct((1, 1), f32),
            jax.ShapeDtypeStruct((fi, ds), f32),
            jax.ShapeDtypeStruct((ft, ds), f32),
        ],
        in_specs=[vmem] + [hbm] * 3,
        out_specs=[vmem] + [hbm] * 2,
        scratch_shapes=[pltpu.VMEM(h.shape, h.dtype) for h in held[1:]]
        + [
            pltpu.VMEM((fi, ds), f32),
            pltpu.VMEM((ft, ds), f32),
            pltpu.SemaphoreType.DMA((4,)),
            pltpu.SemaphoreType.DMA((pl.cdiv(fi, LANES * 2) + pl.cdiv(ft, LANES * 2),)),
        ],
        compiler_params=pltpu.CompilerParams(vmem_limit_bytes=FUSED_VMEM_BYTES),
        name="weight_grads",
    )(*held)
    return (loss.reshape(()), grad_img, grad_txt)


def fits(n_img, n_txt, image, text, t_img, t_txt, proj_img, proj_txt):
    rows, fi = image.shape
    batch = rows * n_img * n_txt
    ft, dt, ds = text.shape[1], t_img.shape[1], proj_img.shape[1]
    half = (fi + ft) // 2
    held = 2 * batch * (fi + ft) + 12 * batch * ds + 16 * batch * batch + 6 * ds * (fi + ft)
    aligned = rows % 16 == 0 and rows * n_img == LANES and rows * n_txt * 2 <= LANES and ft % 128 == 0 and dt % 128 == 0
    aligned = aligned and fi % 128 == 0 and (fi + ft) % 256 == 0 and half < fi and (rows * n_txt) % 32 == 0
    return n_txt == 4 and n_img % 2 == 0 and n_img > 2 and aligned and held <= FUSED_VMEM_BYTES * 3 // 4


def solution(mesh):
    n_img, n_txt = mesh.shape["img"], mesh.shape["txt"]

    def per_device(*arrays):
        if fits(n_img, n_txt, *arrays):
            return whole_batch(n_img, n_txt, *arrays)
        return shards(*arrays)

    return jax.shard_map(
        per_device,
        mesh=mesh,
        in_specs=(
            P(("img", "txt"), None),
            P(("txt", "img"), None),
            P(("img", "txt"), None),
            P(("txt", "img"), None),
            P(),
            P(),
        ),
        out_specs=(P(), P(), P()),
        check_vma=False,
    )
```

```python
import functools

import jax
import jax.numpy as jnp
from jax import lax
from jax.experimental import pallas as pl
from jax.experimental.pallas import tpu as pltpu
from jax.sharding import PartitionSpec as P

EPS = 1e-06
TEACHER_SCALE = 100.0
STUDENT_SCALE = 50.0


def project(feats, weight):
    u = jnp.dot(feats, weight, preferred_element_type=jnp.float32)
    inv = lax.rsqrt(jnp.sum(u * u, axis=1, keepdims=True) + EPS)
    return (u * inv, inv)


def normed(raw):
    x = raw.astype(jnp.float32)
    return (x * lax.rsqrt(jnp.sum(x * x, axis=1, keepdims=True) + EPS)).astype(jnp.bfloat16)


def tangent(grad_rows, embeds, inverse):
    return (grad_rows - embeds * jnp.sum(embeds * grad_rows, 1, keepdims=True)) * inverse


def weight_grad(feats, du_rows):
    return lax.dot_general(
        feats.astype(jnp.float32),
        du_rows,
        (((0,), (0,)), ((), ())),
        precision=lax.Precision.HIGHEST,
    )


def tile_terms(block_q_img, block_q_txt, block_s_img, block_s_txt):
    tl = TEACHER_SCALE * jnp.dot(block_q_img, block_q_txt.T, preferred_element_type=jnp.float32)
    sl = STUDENT_SCALE * jnp.dot(block_s_img, block_s_txt.T, preferred_element_type=jnp.float32)
    rtm, rsm = lax.pmax((tl.max(1), sl.max(1)), "txt")
    rts, rss = lax.psum(
        (jnp.sum(jnp.exp(tl - rtm[:, None]), 1), jnp.sum(jnp.exp(sl - rsm[:, None]), 1)), "txt"
    )
    ctm, csm = lax.pmax((tl.max(0), sl.max(0)), "img")
    cts, css = lax.psum(
        (jnp.sum(jnp.exp(tl - ctm[None, :]), 0), jnp.sum(jnp.exp(sl - csm[None, :]), 0)), "img"
    )
    pt_row = jnp.exp(tl - rtm[:, None]) / rts[:, None]
    ps_row = jnp.exp(sl - rsm[:, None]) / rss[:, None]
    pt_col = jnp.exp(tl - ctm[None, :]) / cts[None, :]
    ps_col = jnp.exp(sl - csm[None, :]) / css[None, :]
    diff = tl - sl
    n_img = lax.axis_size("img")
    n_txt = lax.axis_size("txt")
    local_term = jnp.sum(pt_row * diff) + jnp.sum(pt_col * diff)
    local_term = local_term + jnp.sum(rsm + jnp.log(rss) - rtm - jnp.log(rts)) / n_txt
    local_term = local_term + jnp.sum(csm + jnp.log(css) - ctm - jnp.log(cts)) / n_img
    grad_tile = (0.5 * STUDENT_SCALE * (ps_row - pt_row + (ps_col - pt_col))).astype(jnp.bfloat16)
    part_img = jnp.dot(grad_tile, block_s_txt, preferred_element_type=jnp.float32)
    part_txt = lax.dot_general(
        grad_tile, block_s_img, (((0,), (0,)), ((), ())), preferred_element_type=jnp.float32
    )
    return (part_img, part_txt, local_term)


def shards(image_feats, text_feats, teacher_img, teacher_txt, proj_img, proj_txt):
    e_img, inv_img = project(image_feats, proj_img)
    e_txt, inv_txt = project(text_feats, proj_txt)
    q_img = normed(teacher_img)
    q_txt = normed(teacher_txt)
    feats_img, block_q_img = (
        lax.all_gather(image_feats, "txt", axis=0, tiled=True),
        lax.all_gather(q_img, "txt", axis=0, tiled=True),
    )
    feats_txt, block_q_txt = (
        lax.all_gather(text_feats, "img", axis=0, tiled=True),
        lax.all_gather(q_txt, "img", axis=0, tiled=True),
    )
    block_s_img = project(feats_img, proj_img)[0].astype(jnp.bfloat16)
    block_s_txt = project(feats_txt, proj_txt)[0].astype(jnp.bfloat16)
    part_img, part_txt, local_term = tile_terms(block_q_img, block_q_txt, block_s_img, block_s_txt)
    d_img = lax.psum_scatter(part_img, "txt", scatter_dimension=0, tiled=True)
    d_txt = lax.psum_scatter(part_txt, "img", scatter_dimension=0, tiled=True)
    local_img = weight_grad(image_feats, tangent(d_img, e_img, inv_img))
    local_txt = weight_grad(text_feats, tangent(d_txt, e_txt, inv_txt))
    grad_img, grad_txt, total = lax.psum((local_img, local_txt, local_term), ("img", "txt"))
    batch_total = image_feats.shape[0] * lax.axis_size("img") * lax.axis_size("txt")
    loss = total / (2.0 * batch_total)
    return (loss, grad_img, grad_txt)


MESH = pl.DeviceIdType.MESH
FUSED_VMEM_BYTES = 60 * 1024 * 1024
LANES = 128


def dot_nt(a, b):
    return lax.dot_general(a, b, (((1,), (1,)), ((), ())), preferred_element_type=jnp.float32)


def dot_tn(a, b):
    return lax.dot_general(a, b, (((0,), (0,)), ((), ())), preferred_element_type=jnp.float32)


def bf16_pieces(x):
    high = x.astype(jnp.bfloat16).astype(jnp.float32)
    middle = (x - high).astype(jnp.bfloat16).astype(jnp.float32)
    return [high, middle, x - high - middle]


def at_places(index, values):
    out = jnp.zeros(index.shape, jnp.float32)
    for i, value in enumerate(values):
        out = jnp.where(index == i, value, out)
    return out.astype(jnp.bfloat16)


class Spread:
    def __init__(self, place, buf, halves, sems, log, straight=False, columns=False):
        self.place, self.buf, self.halves, self.log = place, buf, halves, log
        self.straight, self.columns = straight, columns
        self.sz, self.rz, self.sx, self.rx, self.sy, self.ry, self.sc, self.rc, self.sd, self.rd, self.se, self.re = sems

    def ref(self, at, part):
        if part is None:
            return self.buf.at[at]
        lo, hi = self.halves[part]
        if self.columns:
            return self.buf.at[at, :, lo:hi]
        return self.buf.at[at, lo:hi]

    def copy(self, at, part, peer, ssem, rsem):
        ref = self.ref(at, part)
        return pltpu.make_async_remote_copy(
            src_ref=ref, dst_ref=ref, send_sem=ssem, recv_sem=rsem, device_id=peer, device_id_type=MESH
        )

    def send(self, *args):
        copy = self.copy(*args)
        copy.start()
        self.log.append(copy)

    def arrived(self, at, part, ssem, rsem):
        self.copy(at, part, self.place.partner, ssem, rsem).wait_recv()

    def own_z(self):
        p = self.place
        for k in range(1, p.nz):
            self.send(p.slot(p.img, p.txt), None, p.z_peer(k), self.sz.at[k - 1], self.rz.at[k - 1])

    def line(self, k):
        p = self.place
        at = p.slot(p.source(k), p.txt)
        if k > 0:
            self.arrived(at, None, self.sz.at[k - 1], self.rz.at[k - 1])
        self.send(at, None, (p.img, p.x_txt), self.sx.at[k], self.rx.at[k])
        self.send(at, None, (p.img, p.y_txt), self.sy.at[k], self.ry.at[k])
        if self.straight:
            self.send(at, None, (p.img, p.d_txt), self.sd.at[0, k], self.rd.at[0, k])
        self.send(at, None, p.partner, self.sc.at[0, k], self.rc.at[0, k])

    def turn(self, k):
        p = self.place
        at = p.slot(p.source(k), p.x_txt)
        self.arrived(at, None, self.sx.at[k], self.rx.at[k])
        if not self.straight:
            self.send(at, 0, (p.img, p.y_txt), self.sd.at[0, k], self.rd.at[0, k])
        self.send(at, None, p.partner, self.sc.at[1, k], self.rc.at[1, k])
        at = p.slot(p.source(k), p.y_txt)
        self.arrived(at, None, self.sy.at[k], self.ry.at[k])
        if not self.straight:
            self.send(at, 1, (p.img, p.x_txt), self.sd.at[1, k], self.rd.at[1, k])
        self.send(at, None, p.partner, self.sc.at[2, k], self.rc.at[2, k])

    def last(self, k):
        p = self.place
        at = p.slot(p.source(k), p.d_txt)
        for i, part in self.parts():
            self.arrived(at, part, self.sd.at[i, k], self.rd.at[i, k])
            self.send(at, part, p.partner, self.se.at[i, k], self.re.at[i, k])

    def parts(self):
        return ((0, None),) if self.straight else ((0, 0), (1, 1))

    def whole(self, which):
        p = self.place
        for k in range(p.nz):
            source = p.other_source(k)
            if which < 3:
                at = p.slot(source, (p.txt, p.x_txt, p.y_txt)[which])
                self.arrived(at, None, self.sc.at[which, k], self.rc.at[which, k])
            else:
                for i, part in self.parts():
                    self.arrived(p.slot(source, p.d_txt), part, self.se.at[i, k], self.re.at[i, k])


class Place:
    def __init__(self, n_img, n_txt):
        self.n_img, self.n_txt, self.nz = n_img, n_txt, n_img // 2
        self.img, self.txt = lax.axis_index("img"), lax.axis_index("txt")
        self.other = self.img + 1 - 2 * lax.rem(self.img, 2)
        self.partner = (self.other, self.txt)
        self.x_txt = self.txt + 1 - 2 * lax.rem(self.txt, 2)
        self.y_txt = lax.rem(self.txt + 2, 4)
        self.d_txt = lax.rem(self.x_txt + 2, 4)

    def slot(self, img, txt):
        return txt * self.n_img + img

    def source(self, k):
        return lax.rem(self.img + self.n_img - 2 * k, self.n_img)

    def other_source(self, k):
        return lax.rem(self.other + self.n_img - 2 * k, self.n_img)

    def z_peer(self, k):
        return (lax.rem(self.img + 2 * k, self.n_img), self.txt)

    def img_at(self, k):
        return lax.rem(self.img + k, self.n_img)

    def txt_at(self, k):
        return lax.rem(self.txt + k, self.n_txt)


def exchange_kernel(n_img, n_txt, image, text, t_img, t_txt, p_img, p_txt, *refs):
    loss, feats_out, du_img_out, du_txt_out = refs[:4]
    feats, tiles, embeds, sl, ps, du_img, du_txt = refs[4:11]
    raw, q_img, q_txt, tile, row_st, col_st, w_img, w_txt, g_tile, load = refs[11:21]
    tz_s, tz_r, tc_s, tc_r, ti_s, ti_r, rs_s, rs_r, cs_s, cs_r = refs[21:31]
    f_sems, p_sems, e_sems = refs[31:43], refs[43:55], refs[55:67]
    p = Place(n_img, n_txt)
    nz, img, txt = p.nz, p.img, p.txt
    rows, fi = image.shape
    ft, dt, ds = text.shape[1], t_img.shape[1], p_img.shape[1]
    half = feats.shape[3]
    batch = sl.shape[0]
    mine = p.slot(img, txt)

    loads = [
        pltpu.make_async_copy(t_img, raw.at[0], load.at[0]),
        pltpu.make_async_copy(t_txt, raw.at[1], load.at[1]),
        pltpu.make_async_copy(image.at[:, 0:half], feats.at[mine, 0], load.at[2]),
        pltpu.make_async_copy(image.at[:, half:fi], feats.at[mine, 1, :, 0 : fi - half], load.at[3]),
        pltpu.make_async_copy(text, feats.at[mine, 1, :, fi - half : half], load.at[4]),
        pltpu.make_async_copy(p_img, w_img, load.at[5]),
        pltpu.make_async_copy(p_txt, w_txt, load.at[6]),
    ]
    for copy in loads:
        copy.start()
    peers = [(p.img_at(k), txt) for k in range(1, n_img)] + [(img, p.txt_at(k)) for k in range(1, n_txt)]
    barrier = pltpu.get_barrier_semaphore()
    for peer in peers:
        pl.semaphore_signal(barrier, inc=1, device_id=peer, device_id_type=MESH)
    loads[0].wait()
    q_img[txt] = normed(raw[0])
    loads[1].wait()
    q_txt[img] = normed(raw[1])
    for copy in loads[2:]:
        copy.wait()
    own = feats[mine, 1]
    e, inv = project(jnp.concatenate([feats[mine, 0], own[:, 0 : fi - half]], axis=1), w_img[...])
    embeds[mine, :, 0:ds] = e.astype(jnp.bfloat16)
    pieces = bf16_pieces(inv)
    e, inv = project(own[:, fi - half : half], w_txt[...])
    embeds[mine, :, ds + LANES :] = e.astype(jnp.bfloat16)
    lane = lax.broadcasted_iota(jnp.int32, (rows, LANES), 1)
    embeds[mine, :, ds : ds + LANES] = at_places(lane, pieces + bf16_pieces(inv))
    pl.semaphore_wait(barrier, len(peers))

    log = []

    def copy_of(ref, peer, ssem, rsem):
        return pltpu.make_async_remote_copy(
            src_ref=ref, dst_ref=ref, send_sem=ssem, recv_sem=rsem, device_id=peer, device_id_type=MESH
        )

    def send(*args):
        copy = copy_of(*args)
        copy.start()
        log.append(copy)

    def arrived(ref, ssem, rsem):
        copy_of(ref, p.partner, ssem, rsem).wait_recv()

    f = Spread(p, feats, ((0, 1), (1, 2)), f_sems, log)
    e = Spread(p, embeds, ((0, ds + LANES), (ds + LANES, 2 * ds + LANES)), e_sems, log, columns=True)
    rows_in, cols_in = rows * n_txt, rows * n_img
    g = Spread(p, tiles, ((0, rows_in // 2), (rows_in // 2, rows_in + 16)), p_sems, log, straight=True)

    for k in range(1, nz):
        send(q_txt.at[img], p.z_peer(k), tz_s.at[k - 1], tz_r.at[k - 1])
    for k in range(1, n_txt):
        send(q_img.at[txt], (img, p.txt_at(k)), ti_s.at[k - 1], ti_r.at[k - 1])
    send(q_txt.at[img], p.partner, tc_s.at[0], tc_r.at[0])
    e.line(0)
    for copy in log[: nz - 1]:
        copy.wait_send()
    del log[: nz - 1]
    e.own_z()
    for k in range(1, nz):
        arrived(q_txt.at[p.source(k)], tz_s.at[k - 1], tz_r.at[k - 1])
        send(q_txt.at[p.source(k)], p.partner, tc_s.at[k], tc_r.at[k])
    for k in range(1, n_txt):
        arrived(q_img.at[p.txt_at(n_txt - k)], ti_s.at[k - 1], ti_r.at[k - 1])
    for k in range(nz):
        arrived(q_txt.at[p.other_source(k)], tc_s.at[k], tc_r.at[k])

    t = TEACHER_SCALE * dot_nt(q_img[...].reshape(rows_in, dt), q_txt[...].reshape(cols_in, dt))
    tile[...] = t
    m = jnp.max(t, axis=1, keepdims=True)
    s = jnp.sum(jnp.exp(t - m), axis=1, keepdims=True)
    lane = lax.broadcasted_iota(jnp.int32, (rows_in, cols_in), 1)
    packed = jnp.where(lane < rows_in, m, s).T
    row_st[txt] = jnp.zeros(row_st.shape[1:], jnp.float32)
    row_st[txt, 0:1, 0:rows_in] = packed[0:1, :]
    row_st[txt, 1:2, 0:rows_in] = packed[rows_in : rows_in + 1, :]
    m = jnp.max(t, axis=0, keepdims=True)
    col_st[img] = jnp.zeros(col_st.shape[1:], jnp.float32)
    col_st[img, 0:1, :] = m
    col_st[img, 1:2, :] = jnp.sum(jnp.exp(t - m), axis=0, keepdims=True)
    for k in range(1, n_img):
        send(col_st.at[img], (p.img_at(k), txt), cs_s.at[k - 1], cs_r.at[k - 1])
    for k in range(1, n_txt):
        send(row_st.at[txt], (img, p.txt_at(k)), rs_s.at[k - 1], rs_r.at[k - 1])

    for k in range(1, nz):
        e.line(k)
    f.own_z()
    for k in range(1, n_img):
        arrived(col_st.at[p.img_at(n_img - k)], cs_s.at[k - 1], cs_r.at[k - 1])
    for k in range(1, n_txt):
        arrived(row_st.at[p.txt_at(n_txt - k)], rs_s.at[k - 1], rs_r.at[k - 1])

    def log_sum(stats):
        m = jnp.max(stats[:, 0, :], axis=0, keepdims=True)
        return m + jnp.log(jnp.sum(stats[:, 1, :] * jnp.exp(stats[:, 0, :] - m), axis=0, keepdims=True))

    lz_row = log_sum(row_st[:, :, 0:rows_in])
    lz_col = log_sum(col_st[...])
    t = tile[...]
    both = jnp.exp(t - jnp.broadcast_to(lz_row, (cols_in, rows_in)).T) + jnp.exp(t - lz_col)
    part = jnp.sum(both * t, axis=0, keepdims=True) - lz_col / n_img
    part = part - jnp.sum(lz_row, axis=1, keepdims=True) / (n_txt * cols_in)
    line = lax.broadcasted_iota(jnp.int32, (16, cols_in), 0)
    tiles[mine, 0:rows_in, :] = both.astype(jnp.bfloat16)
    tiles[mine, rows_in : rows_in + 16, :] = at_places(line, bf16_pieces(part))
    g.own_z()
    g.line(0)

    for k in range(nz):
        e.turn(k)
    f.line(0)
    for k in range(1, nz):
        g.line(k)
    for k in range(nz):
        e.last(k)
    for k in range(1, nz):
        f.line(k)
    for which in range(4):
        e.whole(which)

    def s_img(c):
        return embeds[c * n_img : (c + 1) * n_img, :, 0:ds].reshape(cols_in, ds)

    def s_txt(c):
        return embeds[c * n_img : (c + 1) * n_img, :, ds + LANES :].reshape(cols_in, ds)

    def inverse(c, at):
        held = embeds[c * n_img : (c + 1) * n_img, :, ds : ds + LANES].reshape(cols_in, LANES).astype(jnp.float32)
        return held[:, at : at + 1] + held[:, at + 1 : at + 2] + held[:, at + 2 : at + 3]

    def all_txt():
        return embeds[:, :, ds + LANES :].reshape(batch, ds)

    chunks = [slice(c * cols_in, (c + 1) * cols_in) for c in range(n_txt)]
    csm = jnp.full((1, batch), -jnp.inf, jnp.float32)
    total = jnp.zeros((1, 1), jnp.float32)
    for c, at in enumerate(chunks):
        s = STUDENT_SCALE * dot_nt(s_img(c), all_txt())
        sl[at, :] = s
        m = jnp.max(s, axis=1, keepdims=True)
        es = jnp.exp(s - m)
        sums = jnp.sum(es, axis=1, keepdims=True)
        ps[at, :] = es * (1.0 / sums)
        total = total + jnp.sum(m + jnp.log(sums), axis=0, keepdims=True)
        csm = jnp.maximum(csm, jnp.max(s, axis=0, keepdims=True))
    css = jnp.zeros((1, batch), jnp.float32)
    for at in chunks:
        css = css + jnp.sum(jnp.exp(sl[at, :] - csm), axis=0, keepdims=True)
    lzc = csm + jnp.log(css)
    total = total + jnp.sum(lzc, axis=1, keepdims=True)
    for at in chunks:
        ps[at, :] = ps[at, :] + jnp.exp(sl[at, :] - lzc)
    for k in range(nz):
        g.turn(k)
    for k in range(nz):
        g.last(k)
    for k in range(nz):
        f.turn(k)
    for copy in log:
        copy.wait_send()
    del log[:]
    for which in range(4):
        g.whole(which)

    def tile_rows(c):
        held = [tiles[i * n_img : (i + 1) * n_img, c * rows : (c + 1) * rows, :] for i in range(n_txt)]
        return jnp.concatenate([h.reshape(cols_in, cols_in) for h in held], axis=1).astype(jnp.float32)

    terms = jnp.zeros((1, batch), jnp.float32)
    for c, at in enumerate(chunks):
        pt = tile_rows(c)
        tile_g = (0.5 * STUDENT_SCALE * (ps[at, :] - pt)).astype(jnp.bfloat16)
        g_tile[at, :] = tile_g
        terms = terms - jnp.sum(pt * sl[at, :], axis=0, keepdims=True)
        d_img = jnp.dot(tile_g, all_txt(), preferred_element_type=jnp.float32)
        du_img[at, :] = tangent(d_img, s_img(c).astype(jnp.float32), inverse(c, 0)).astype(jnp.bfloat16)
    outs = [pltpu.make_async_copy(du_img, du_img_out, load.at[1])]
    outs[0].start()
    for k in range(nz):
        f.last(k)
    for c, at in enumerate(chunks):
        d_txt = dot_tn(g_tile[:, at], embeds[:, :, 0:ds].reshape(batch, ds))
        du_txt[at, :] = tangent(d_txt, s_txt(c).astype(jnp.float32), inverse(c, 3)).astype(jnp.bfloat16)
    outs.append(pltpu.make_async_copy(du_txt, du_txt_out, load.at[2]))
    outs[1].start()
    for which in range(4):
        f.whole(which)
    outs.append(pltpu.make_async_copy(feats, feats_out, load.at[0]))
    outs[2].start()
    parts = jnp.sum(tiles[:, rows_in : rows_in + 16, :].astype(jnp.float32), axis=0)
    total = total + jnp.sum(terms, axis=1, keepdims=True)
    total = total + jnp.sum(jnp.sum(parts, axis=0, keepdims=True), axis=1, keepdims=True)
    loss[...] = total / (2.0 * batch)
    for copy in log:
        copy.wait_send()
    for copy in outs:
        copy.wait()


def exchange(n_img, n_txt, image, text, t_img, t_txt, w_img, w_txt):
    rows, fi = image.shape
    ft, dt, ds = text.shape[1], t_img.shape[1], w_img.shape[1]
    nz, slots = n_img // 2, n_img * n_txt
    batch, rows_in, cols_in = rows * slots, rows * n_txt, rows * n_img
    f32, b16 = jnp.float32, jnp.bfloat16
    dma = pltpu.SemaphoreType.DMA
    vmem = pl.BlockSpec(memory_space=pltpu.VMEM)
    hbm = pl.BlockSpec(memory_space=pltpu.HBM)
    outs = [((1, 1), f32), ((slots, 2, rows, (fi + ft) // 2), b16), ((batch, ds), b16), ((batch, ds), b16)]
    held = [
        ((slots, 2, rows, (fi + ft) // 2), b16),
        ((slots, rows_in + 16, cols_in), b16),
        ((slots, rows, 2 * ds + LANES), b16),
        ((batch, batch), f32),
        ((batch, batch), f32),
        ((batch, ds), b16),
        ((batch, ds), b16),
    ]
    scratch = [pltpu.VMEM(*h) for h in held] + [
        pltpu.VMEM((2, rows, dt), b16),
        pltpu.VMEM((n_txt, rows, dt), b16),
        pltpu.VMEM((n_img, rows, dt), b16),
        pltpu.VMEM((rows_in, cols_in), f32),
        pltpu.VMEM((n_txt, 8, LANES), f32),
        pltpu.VMEM((n_img, 8, LANES), f32),
        pltpu.VMEM((fi, ds), b16),
        pltpu.VMEM((ft, ds), b16),
        pltpu.VMEM((batch, batch), b16),
        dma((7,)),
    ]
    spread = [(nz - 1,), (nz,), (nz,), (3, nz), (2, nz), (2, nz)]
    for shape in [(nz - 1,), (nz,), (n_txt - 1,), (n_txt - 1,), (n_img - 1,)] + spread * 3:
        scratch += [dma(shape), dma(shape)]
    return pl.pallas_call(
        functools.partial(exchange_kernel, n_img, n_txt),
        out_shape=[jax.ShapeDtypeStruct(*s) for s in outs],
        in_specs=[hbm] * 6,
        out_specs=[vmem] + [hbm] * 3,
        scratch_shapes=scratch,
        compiler_params=pltpu.CompilerParams(
            collective_id=0, has_side_effects=True, vmem_limit_bytes=FUSED_VMEM_BYTES
        ),
        name="embed_and_exchange",
    )(image, text, t_img, t_txt, w_img, w_txt)


def grads_kernel(loss_in, feats_in, du_img_in, du_txt_in, loss, grad_img, grad_txt, feats, du_img, du_txt, g_img, g_txt, load, store):
    slots, _, rows, half = feats.shape
    batch = slots * rows
    fi, ft = grad_img.shape[0], grad_txt.shape[0]
    step = LANES * 2
    loads = [
        pltpu.make_async_copy(du_img_in, du_img, load.at[0]),
        pltpu.make_async_copy(feats_in.at[:, 0], feats.at[:, 0], load.at[1]),
        pltpu.make_async_copy(feats_in.at[:, 1], feats.at[:, 1], load.at[2]),
        pltpu.make_async_copy(du_txt_in, du_txt, load.at[3]),
    ]
    for copy in loads:
        copy.start()
    loss[...] = loss_in[...]
    stores = []

    def block(part, lo, hi, at, du, held, out):
        here = slice(at, at + hi - lo)
        held[here, :] = dot_tn(feats[:, part, :, lo:hi].reshape(batch, hi - lo), du[...])
        copy = pltpu.make_async_copy(held.at[here], out.at[here], store.at[len(stores)])
        copy.start()
        stores.append(copy)

    for copy in loads[:2]:
        copy.wait()
    for lo in range(0, half, step):
        block(0, lo, min(lo + step, half), lo, du_img, g_img, grad_img)
    loads[2].wait()
    block(1, 0, fi - half, half, du_img, g_img, grad_img)
    loads[3].wait()
    for lo in range(0, ft, step):
        block(1, fi - half + lo, fi - half + min(lo + step, ft), lo, du_txt, g_txt, grad_txt)
    for copy in stores:
        copy.wait()


def whole_batch(n_img, n_txt, image_feats, text_feats, teacher_img, teacher_txt, proj_img, proj_txt):
    held = exchange(n_img, n_txt, image_feats, text_feats, teacher_img, teacher_txt, proj_img, proj_txt)
    (fi, ds), ft = proj_img.shape, proj_txt.shape[0]
    vmem = pl.BlockSpec(memory_space=pltpu.VMEM)
    hbm = pl.BlockSpec(memory_space=pltpu.HBM)
    f32 = jnp.float32
    loss, grad_img, grad_txt = pl.pallas_call(
        grads_kernel,
        out_shape=[
            jax.ShapeDtypeStruct((1, 1), f32),
            jax.ShapeDtypeStruct((fi, ds), f32),
            jax.ShapeDtypeStruct((ft, ds), f32),
        ],
        in_specs=[vmem] + [hbm] * 3,
        out_specs=[vmem] + [hbm] * 2,
        scratch_shapes=[pltpu.VMEM(h.shape, h.dtype) for h in held[1:]]
        + [
            pltpu.VMEM((fi, ds), f32),
            pltpu.VMEM((ft, ds), f32),
            pltpu.SemaphoreType.DMA((4,)),
            pltpu.SemaphoreType.DMA((pl.cdiv(held[1].shape[3], LANES * 2) + 1 + pl.cdiv(ft, LANES * 2),)),
        ],
        compiler_params=pltpu.CompilerParams(vmem_limit_bytes=FUSED_VMEM_BYTES),
        name="weight_grads",
    )(*held)
    return (loss.reshape(()), grad_img, grad_txt)


def fits(n_img, n_txt, image, text, t_img, t_txt, proj_img, proj_txt):
    rows, fi = image.shape
    batch = rows * n_img * n_txt
    ft, dt, ds = text.shape[1], t_img.shape[1], proj_img.shape[1]
    half = (fi + ft) // 2
    held = 2 * batch * (fi + ft) + 12 * batch * ds + 16 * batch * batch + 6 * ds * (fi + ft)
    aligned = rows % 16 == 0 and rows * n_img == LANES and rows * n_txt * 2 <= LANES and ft % 128 == 0 and dt % 128 == 0
    aligned = aligned and fi % 128 == 0 and (fi + ft) % 256 == 0 and half < fi and (rows * n_txt) % 32 == 0
    return n_txt == 4 and n_img % 2 == 0 and n_img > 2 and aligned and held <= FUSED_VMEM_BYTES * 3 // 4


def solution(mesh):
    n_img, n_txt = mesh.shape["img"], mesh.shape["txt"]

    def per_device(*arrays):
        if fits(n_img, n_txt, *arrays):
            return whole_batch(n_img, n_txt, *arrays)
        return shards(*arrays)

    return jax.shard_map(
        per_device,
        mesh=mesh,
        in_specs=(
            P(("img", "txt"), None),
            P(("txt", "img"), None),
            P(("img", "txt"), None),
            P(("txt", "img"), None),
            P(),
            P(),
        ),
        out_specs=(P(), P(), P()),
        check_vma=False,
    )
```

```python
import functools

import jax
import jax.numpy as jnp
from jax import lax
from jax.experimental import pallas as pl
from jax.experimental.pallas import tpu as pltpu
from jax.sharding import PartitionSpec as P

EPS = 1e-06
TEACHER_SCALE = 100.0
STUDENT_SCALE = 50.0


def project(feats, weight):
    u = jnp.dot(feats, weight, preferred_element_type=jnp.float32)
    inv = lax.rsqrt(jnp.sum(u * u, axis=1, keepdims=True) + EPS)
    return (u * inv, inv)


def normed(raw):
    x = raw.astype(jnp.float32)
    return (x * lax.rsqrt(jnp.sum(x * x, axis=1, keepdims=True) + EPS)).astype(jnp.bfloat16)


def tangent(grad_rows, embeds, inverse):
    return (grad_rows - embeds * jnp.sum(embeds * grad_rows, 1, keepdims=True)) * inverse


def weight_grad(feats, du_rows):
    return lax.dot_general(
        feats.astype(jnp.float32),
        du_rows,
        (((0,), (0,)), ((), ())),
        precision=lax.Precision.HIGHEST,
    )


def tile_terms(block_q_img, block_q_txt, block_s_img, block_s_txt):
    tl = TEACHER_SCALE * jnp.dot(block_q_img, block_q_txt.T, preferred_element_type=jnp.float32)
    sl = STUDENT_SCALE * jnp.dot(block_s_img, block_s_txt.T, preferred_element_type=jnp.float32)
    rtm, rsm = lax.pmax((tl.max(1), sl.max(1)), "txt")
    rts, rss = lax.psum(
        (jnp.sum(jnp.exp(tl - rtm[:, None]), 1), jnp.sum(jnp.exp(sl - rsm[:, None]), 1)), "txt"
    )
    ctm, csm = lax.pmax((tl.max(0), sl.max(0)), "img")
    cts, css = lax.psum(
        (jnp.sum(jnp.exp(tl - ctm[None, :]), 0), jnp.sum(jnp.exp(sl - csm[None, :]), 0)), "img"
    )
    pt_row = jnp.exp(tl - rtm[:, None]) / rts[:, None]
    ps_row = jnp.exp(sl - rsm[:, None]) / rss[:, None]
    pt_col = jnp.exp(tl - ctm[None, :]) / cts[None, :]
    ps_col = jnp.exp(sl - csm[None, :]) / css[None, :]
    diff = tl - sl
    n_img = lax.axis_size("img")
    n_txt = lax.axis_size("txt")
    local_term = jnp.sum(pt_row * diff) + jnp.sum(pt_col * diff)
    local_term = local_term + jnp.sum(rsm + jnp.log(rss) - rtm - jnp.log(rts)) / n_txt
    local_term = local_term + jnp.sum(csm + jnp.log(css) - ctm - jnp.log(cts)) / n_img
    grad_tile = (0.5 * STUDENT_SCALE * (ps_row - pt_row + (ps_col - pt_col))).astype(jnp.bfloat16)
    part_img = jnp.dot(grad_tile, block_s_txt, preferred_element_type=jnp.float32)
    part_txt = lax.dot_general(
        grad_tile, block_s_img, (((0,), (0,)), ((), ())), preferred_element_type=jnp.float32
    )
    return (part_img, part_txt, local_term)


def shards(image_feats, text_feats, teacher_img, teacher_txt, proj_img, proj_txt):
    e_img, inv_img = project(image_feats, proj_img)
    e_txt, inv_txt = project(text_feats, proj_txt)
    q_img = normed(teacher_img)
    q_txt = normed(teacher_txt)
    feats_img, block_q_img = (
        lax.all_gather(image_feats, "txt", axis=0, tiled=True),
        lax.all_gather(q_img, "txt", axis=0, tiled=True),
    )
    feats_txt, block_q_txt = (
        lax.all_gather(text_feats, "img", axis=0, tiled=True),
        lax.all_gather(q_txt, "img", axis=0, tiled=True),
    )
    block_s_img = project(feats_img, proj_img)[0].astype(jnp.bfloat16)
    block_s_txt = project(feats_txt, proj_txt)[0].astype(jnp.bfloat16)
    part_img, part_txt, local_term = tile_terms(block_q_img, block_q_txt, block_s_img, block_s_txt)
    d_img = lax.psum_scatter(part_img, "txt", scatter_dimension=0, tiled=True)
    d_txt = lax.psum_scatter(part_txt, "img", scatter_dimension=0, tiled=True)
    local_img = weight_grad(image_feats, tangent(d_img, e_img, inv_img))
    local_txt = weight_grad(text_feats, tangent(d_txt, e_txt, inv_txt))
    grad_img, grad_txt, total = lax.psum((local_img, local_txt, local_term), ("img", "txt"))
    batch_total = image_feats.shape[0] * lax.axis_size("img") * lax.axis_size("txt")
    loss = total / (2.0 * batch_total)
    return (loss, grad_img, grad_txt)


MESH = pl.DeviceIdType.MESH
FUSED_VMEM_BYTES = 60 * 1024 * 1024
LANES = 128


def dot_nt(a, b):
    return lax.dot_general(a, b, (((1,), (1,)), ((), ())), preferred_element_type=jnp.float32)


def dot_tn(a, b):
    return lax.dot_general(a, b, (((0,), (0,)), ((), ())), preferred_element_type=jnp.float32)


class Spread:
    def __init__(self, place, buf, halves, sems, log, straight=False):
        self.place, self.buf, self.halves, self.log, self.straight = place, buf, halves, log, straight
        self.sz, self.rz, self.sl, self.rl, self.sc, self.rc = sems

    def copy(self, at, part, peer, ssem, rsem):
        if part is None:
            ref = self.buf.at[at]
        else:
            lo, hi = self.halves[part]
            ref = self.buf.at[at, lo:hi]
        return pltpu.make_async_remote_copy(
            src_ref=ref, dst_ref=ref, send_sem=ssem, recv_sem=rsem, device_id=peer, device_id_type=MESH
        )

    def send(self, *args):
        copy = self.copy(*args)
        copy.start()
        self.log.append(copy)

    def arrived(self, at, part, ssem, rsem):
        self.copy(at, part, self.place.partner, ssem, rsem).wait_recv()

    def own_z(self):
        p = self.place
        for k in range(1, p.nz):
            self.send(p.slot(p.img, p.txt), None, p.z_peer(k), self.sz.at[k - 1], self.rz.at[k - 1])

    def line(self):
        p = self.place
        for k in range(1, p.nz):
            self.arrived(p.slot(p.source(k), p.txt), None, self.sz.at[k - 1], self.rz.at[k - 1])
        at = p.line(p.img, p.txt)
        if self.straight:
            self.send(at, None, (p.img, p.d_txt), self.sl.at[2], self.rl.at[2])
        self.send(at, None, (p.img, p.x_txt), self.sl.at[0], self.rl.at[0])
        self.send(at, None, (p.img, p.y_txt), self.sl.at[1], self.rl.at[1])
        self.send(at, None, p.partner, self.sc.at[0], self.rc.at[0])

    def turn(self):
        p = self.place
        for i, (near, far) in enumerate([(p.x_txt, p.y_txt), (p.y_txt, p.x_txt)]):
            at = p.line(p.img, near)
            self.arrived(at, None, self.sl.at[i], self.rl.at[i])
            if not self.straight:
                self.send(at, i, (p.img, far), self.sl.at[2 + i], self.rl.at[2 + i])
            self.send(at, None, p.partner, self.sc.at[1 + i], self.rc.at[1 + i])

    def last(self):
        p = self.place
        at = p.line(p.img, p.d_txt)
        for i, part in self.parts():
            self.arrived(at, part, self.sl.at[2 + i], self.rl.at[2 + i])
        self.send(at, None, p.partner, self.sc.at[3], self.rc.at[3])

    def parts(self):
        return ((0, None),) if self.straight else ((0, 0), (1, 1))

    def whole(self, which):
        p = self.place
        at = p.line(p.other, (p.txt, p.x_txt, p.y_txt, p.d_txt)[which])
        self.arrived(at, None, self.sc.at[which], self.rc.at[which])


class Place:
    def __init__(self, n_img, n_txt):
        self.n_img, self.n_txt, self.nz = n_img, n_txt, n_img // 2
        self.img, self.txt = lax.axis_index("img"), lax.axis_index("txt")
        self.other = self.img + 1 - 2 * lax.rem(self.img, 2)
        self.partner = (self.other, self.txt)
        self.x_txt = self.txt + 1 - 2 * lax.rem(self.txt, 2)
        self.y_txt = lax.rem(self.txt + 2, 4)
        self.d_txt = lax.rem(self.x_txt + 2, 4)

    def order(self, img):
        return lax.rem(img, 2) * self.nz + img // 2

    def slot(self, img, txt):
        return txt * self.n_img + self.order(img)

    def line(self, img, txt):
        return pl.ds(txt * self.n_img + lax.rem(img, 2) * self.nz, self.nz)

    def source(self, k):
        return lax.rem(self.img + self.n_img - 2 * k, self.n_img)

    def other_source(self, k):
        return lax.rem(self.other + self.n_img - 2 * k, self.n_img)

    def z_peer(self, k):
        return (lax.rem(self.img + 2 * k, self.n_img), self.txt)

    def img_at(self, k):
        return lax.rem(self.img + k, self.n_img)

    def txt_at(self, k):
        return lax.rem(self.txt + k, self.n_txt)


def exchange_kernel(n_img, n_txt, image, text, t_img, t_txt, p_img, p_txt, *refs):
    loss_out, turned_out, du_img_out, du_txt_out = refs[:4]
    feats, tiles, e_img, e_txt, i_img, i_txt, s_img, s_txt, sl, ps, du_img, du_txt = refs[4:16]
    turned, loss = refs[48:50]
    raw, q_img, q_txt, tile, row_st, col_st, w_img, w_txt, g_tile, load = refs[16:26]
    tz_s, tz_r, tc_s, tc_r, ti_s, ti_r, rs_s, rs_r, cs_s, cs_r = refs[26:36]
    f_sems, p_sems = refs[36:42], refs[42:48]
    p = Place(n_img, n_txt)
    nz, img, txt = p.nz, p.img, p.txt
    rows, fi = image.shape
    ft, dt = text.shape[1], t_img.shape[1]
    half = feats.shape[3]
    batch = sl.shape[0]
    mine = p.slot(img, txt)

    loads = [
        pltpu.make_async_copy(t_img, raw.at[0], load.at[0]),
        pltpu.make_async_copy(t_txt, raw.at[1], load.at[1]),
        pltpu.make_async_copy(image.at[:, 0:half], feats.at[mine, 0], load.at[2]),
        pltpu.make_async_copy(image.at[:, half:fi], feats.at[mine, 1, :, 0 : fi - half], load.at[3]),
        pltpu.make_async_copy(text, feats.at[mine, 1, :, fi - half : half], load.at[4]),
        pltpu.make_async_copy(p_img, w_img, load.at[5]),
        pltpu.make_async_copy(p_txt, w_txt, load.at[6]),
    ]
    for copy in loads:
        copy.start()
    peers = [(p.img_at(k), txt) for k in range(1, n_img)] + [(img, p.txt_at(k)) for k in range(1, n_txt)]
    barrier = pltpu.get_barrier_semaphore()
    for peer in peers:
        pl.semaphore_signal(barrier, inc=1, device_id=peer, device_id_type=MESH)
    loads[0].wait()
    q_img[txt] = normed(raw[0])
    loads[1].wait()
    mine_q = p.order(img)
    q_txt[mine_q] = normed(raw[1])
    for copy in loads[2:5]:
        copy.wait()
    pl.semaphore_wait(barrier, len(peers))

    log = []

    def copy_of(ref, peer, ssem, rsem):
        return pltpu.make_async_remote_copy(
            src_ref=ref, dst_ref=ref, send_sem=ssem, recv_sem=rsem, device_id=peer, device_id_type=MESH
        )

    def send(*args):
        copy = copy_of(*args)
        copy.start()
        log.append(copy)

    def arrived(ref, ssem, rsem):
        copy_of(ref, p.partner, ssem, rsem).wait_recv()

    f = Spread(p, feats, ((0, 1), (1, 2)), f_sems, log)
    rows_in, cols_in = rows * n_txt, rows * n_img
    g = Spread(p, tiles, ((0, rows_in // 2), (rows_in // 2, rows_in + 16)), p_sems, log, straight=True)

    for k in range(1, nz):
        send(q_txt.at[mine_q], p.z_peer(k), tz_s.at[k - 1], tz_r.at[k - 1])
    for k in range(1, n_txt):
        send(q_img.at[txt], (img, p.txt_at(k)), ti_s.at[k - 1], ti_r.at[k - 1])
    for copy in log[: nz - 1]:
        copy.wait_send()
    del log[: nz - 1]
    f.own_z()
    for k in range(1, nz):
        arrived(q_txt.at[p.order(p.source(k))], tz_s.at[k - 1], tz_r.at[k - 1])
    send(q_txt.at[p.line(img, 0)], p.partner, tc_s.at[0], tc_r.at[0])
    for k in range(1, n_txt):
        arrived(q_img.at[p.txt_at(n_txt - k)], ti_s.at[k - 1], ti_r.at[k - 1])
    arrived(q_txt.at[p.line(p.other, 0)], tc_s.at[0], tc_r.at[0])

    t = TEACHER_SCALE * dot_nt(q_img[...].reshape(rows_in, dt), q_txt[...].reshape(cols_in, dt))
    tile[...] = t
    m = jnp.max(t, axis=1, keepdims=True)
    s = jnp.sum(jnp.exp(t - m), axis=1, keepdims=True)
    lane = lax.broadcasted_iota(jnp.int32, (rows_in, cols_in), 1)
    packed = jnp.where(lane < rows_in, m, s).T
    row_st[txt] = jnp.zeros(row_st.shape[1:], jnp.float32)
    row_st[txt, 0:1, 0:rows_in] = packed[0:1, :]
    row_st[txt, 1:2, 0:rows_in] = packed[rows_in : rows_in + 1, :]
    m = jnp.max(t, axis=0, keepdims=True)
    col_st[img] = jnp.zeros(col_st.shape[1:], jnp.float32)
    col_st[img, 0:1, :] = m
    col_st[img, 1:2, :] = jnp.sum(jnp.exp(t - m), axis=0, keepdims=True)
    for k in range(1, n_img):
        send(col_st.at[img], (p.img_at(k), txt), cs_s.at[k - 1], cs_r.at[k - 1])
    for k in range(1, n_txt):
        send(row_st.at[txt], (img, p.txt_at(k)), rs_s.at[k - 1], rs_r.at[k - 1])

    f.line()
    for k in range(1, n_img):
        arrived(col_st.at[p.img_at(n_img - k)], cs_s.at[k - 1], cs_r.at[k - 1])
    for k in range(1, n_txt):
        arrived(row_st.at[p.txt_at(n_txt - k)], rs_s.at[k - 1], rs_r.at[k - 1])

    def log_sum(stats):
        m = jnp.max(stats[:, 0, :], axis=0, keepdims=True)
        return m + jnp.log(jnp.sum(stats[:, 1, :] * jnp.exp(stats[:, 0, :] - m), axis=0, keepdims=True))

    lz_row = log_sum(row_st[:, :, 0:rows_in])
    lz_col = log_sum(col_st[...])
    t = tile[...]
    both = jnp.exp(t - jnp.broadcast_to(lz_row, (cols_in, rows_in)).T) + jnp.exp(t - lz_col)
    part = jnp.sum(both * t, axis=0, keepdims=True) - lz_col / n_img
    part = part - jnp.sum(lz_row, axis=1, keepdims=True) / (n_txt * cols_in)
    high = part.astype(jnp.bfloat16).astype(jnp.float32)
    middle = (part - high).astype(jnp.bfloat16).astype(jnp.float32)
    line = lax.broadcasted_iota(jnp.int32, (16, cols_in), 0)
    pieces = jnp.where(line == 0, high, jnp.where(line == 1, middle, jnp.where(line == 2, part - high - middle, 0.0)))
    tiles[mine, 0:rows_in, :] = both.astype(jnp.bfloat16)
    tiles[mine, rows_in : rows_in + 16, :] = pieces.astype(jnp.bfloat16)
    g.own_z()

    def embed(j):
        at = pl.ds(pl.multiple_of(j * cols_in, cols_in), cols_in)
        here = pl.ds(j * n_img, n_img)
        rest = feats[here, 1].reshape(cols_in, half)
        x = jnp.concatenate([feats[here, 0].reshape(cols_in, half), rest[:, 0 : fi - half]], axis=1)
        turned[0:fi, at] = x.T
        turned[fi : fi + ft, at] = rest[:, fi - half : half].T
        e, inv = project(x, w_img[...])
        e_img[at, :], i_img[at, :] = e, inv
        s_img[at, :] = e.astype(jnp.bfloat16)
        e, inv = project(rest[:, fi - half : half], w_txt[...])
        e_txt[at, :], i_txt[at, :] = e, inv
        s_txt[at, :] = e.astype(jnp.bfloat16)

    f.turn()
    g.line()
    f.whole(0)
    for copy in loads[5:]:
        copy.wait()
    embed(txt)
    f.whole(1)
    embed(p.x_txt)
    f.last()
    f.whole(2)
    embed(p.y_txt)
    g.turn()
    g.last()
    f.whole(3)
    embed(p.d_txt)
    outs = [pltpu.make_async_copy(turned, turned_out, load.at[0])]
    outs[0].start()

    chunks = [slice(c * cols_in, (c + 1) * cols_in) for c in range(n_txt)]
    csm = jnp.full((1, batch), -jnp.inf, jnp.float32)
    total = jnp.zeros((1, 1), jnp.float32)
    for at in chunks:
        s = STUDENT_SCALE * dot_nt(s_img[at, :], s_txt[...])
        sl[at, :] = s
        m = jnp.max(s, axis=1, keepdims=True)
        es = jnp.exp(s - m)
        sums = jnp.sum(es, axis=1, keepdims=True)
        ps[at, :] = es * (1.0 / sums)
        total = total + jnp.sum(m + jnp.log(sums), axis=0, keepdims=True)
        csm = jnp.maximum(csm, jnp.max(s, axis=0, keepdims=True))
    css = jnp.zeros((1, batch), jnp.float32)
    for at in chunks:
        css = css + jnp.sum(jnp.exp(sl[at, :] - csm), axis=0, keepdims=True)
    lzc = csm + jnp.log(css)
    total = total + jnp.sum(lzc, axis=1, keepdims=True)
    for at in chunks:
        ps[at, :] = ps[at, :] + jnp.exp(sl[at, :] - lzc)
    for copy in log:
        copy.wait_send()
    for which in range(4):
        g.whole(which)

    def tile_rows(c):
        held = [tiles[i * n_img : (i + 1) * n_img, c * rows : (c + 1) * rows, :] for i in range(n_txt)]
        return jnp.concatenate([h.reshape(cols_in, cols_in) for h in held], axis=1).astype(jnp.float32)

    terms = jnp.zeros((1, batch), jnp.float32)
    for c, at in enumerate(chunks):
        pt = tile_rows(c)
        tile_g = (0.5 * STUDENT_SCALE * (ps[at, :] - pt)).astype(jnp.bfloat16)
        g_tile[at, :] = tile_g
        terms = terms - jnp.sum(pt * sl[at, :], axis=0, keepdims=True)
        d_img = jnp.dot(tile_g, s_txt[...], preferred_element_type=jnp.float32)
        du_img[at, :] = tangent(d_img, e_img[at, :], i_img[at, :]).astype(jnp.bfloat16)
    outs.append(pltpu.make_async_copy(du_img, du_img_out, load.at[1]))
    outs[1].start()
    parts = jnp.sum(tiles[:, rows_in : rows_in + 16, :].astype(jnp.float32), axis=0)
    total = total + jnp.sum(terms, axis=1, keepdims=True)
    total = total + jnp.sum(jnp.sum(parts, axis=0, keepdims=True), axis=1, keepdims=True)
    loss[...] = total / (2.0 * batch)
    outs.append(pltpu.make_async_copy(loss, loss_out, load.at[3]))
    outs[2].start()
    for at in chunks:
        d_txt = dot_tn(g_tile[:, at], s_img[...])
        du_txt[at, :] = tangent(d_txt, e_txt[at, :], i_txt[at, :]).astype(jnp.bfloat16)
    outs.append(pltpu.make_async_copy(du_txt, du_txt_out, load.at[2]))
    outs[3].start()
    for copy in outs:
        copy.wait()


def exchange(n_img, n_txt, image, text, t_img, t_txt, w_img, w_txt):
    rows, fi = image.shape
    ft, dt, ds = text.shape[1], t_img.shape[1], w_img.shape[1]
    nz, slots = n_img // 2, n_img * n_txt
    batch, rows_in, cols_in = rows * slots, rows * n_txt, rows * n_img
    f32, b16 = jnp.float32, jnp.bfloat16
    dma = pltpu.SemaphoreType.DMA
    vmem = pl.BlockSpec(memory_space=pltpu.VMEM)
    hbm = pl.BlockSpec(memory_space=pltpu.HBM)
    outs = [((1, 1), f32), ((fi + ft, batch), b16), ((batch, ds), b16), ((batch, ds), b16)]
    held = [
        ((slots, 2, rows, (fi + ft) // 2), b16),
        ((slots, rows_in + 16, cols_in), b16),
        ((batch, ds), f32),
        ((batch, ds), f32),
        ((batch, 1), f32),
        ((batch, 1), f32),
        ((batch, ds), b16),
        ((batch, ds), b16),
        ((batch, batch), f32),
        ((batch, batch), f32),
        ((batch, ds), b16),
        ((batch, ds), b16),
    ]
    scratch = [pltpu.VMEM(*h) for h in held] + [
        pltpu.VMEM((2, rows, dt), b16),
        pltpu.VMEM((n_txt, rows, dt), b16),
        pltpu.VMEM((n_img, rows, dt), b16),
        pltpu.VMEM((rows_in, cols_in), f32),
        pltpu.VMEM((n_txt, 8, LANES), f32),
        pltpu.VMEM((n_img, 8, LANES), f32),
        pltpu.VMEM((fi, ds), b16),
        pltpu.VMEM((ft, ds), b16),
        pltpu.VMEM((batch, batch), b16),
        dma((7,)),
    ]
    spread = [(nz - 1,), (4,), (4,)]
    for shape in [(nz - 1,), (1,), (n_txt - 1,), (n_txt - 1,), (n_img - 1,)] + spread + spread:
        scratch += [dma(shape), dma(shape)]
    scratch += [pltpu.VMEM((fi + ft, batch), b16), pltpu.VMEM((1, 1), f32)]
    return pl.pallas_call(
        functools.partial(exchange_kernel, n_img, n_txt),
        out_shape=[jax.ShapeDtypeStruct(*s) for s in outs],
        in_specs=[hbm] * 6,
        out_specs=[hbm] * 4,
        scratch_shapes=scratch,
        compiler_params=pltpu.CompilerParams(
            collective_id=0, has_side_effects=True, vmem_limit_bytes=FUSED_VMEM_BYTES
        ),
        name="exchange_and_embed",
    )(image, text, t_img, t_txt, w_img, w_txt)


def grads_kernel(loss_in, turned_in, du_img_in, du_txt_in, loss, grad_img, grad_txt, turned, du_img, du_txt, g_img, g_txt, load, store):
    fi, ft = grad_img.shape[0], grad_txt.shape[0]
    step = LANES * 2
    loads = [
        pltpu.make_async_copy(du_img_in, du_img, load.at[0]),
        pltpu.make_async_copy(turned_in.at[0:step], turned.at[0:step], load.at[1]),
        pltpu.make_async_copy(turned_in.at[step : fi + ft], turned.at[step : fi + ft], load.at[2]),
        pltpu.make_async_copy(du_txt_in, du_txt, load.at[3]),
    ]
    for copy in loads:
        copy.start()
    stores = [pltpu.make_async_copy(loss_in, loss, store.at[0])]
    stores[0].start()

    def block(lo, at, du, held, out):
        rows = min(step, held.shape[0] - at)
        here = slice(at, at + rows)
        held[here, :] = jnp.dot(turned[lo + at : lo + at + rows, :], du[...], preferred_element_type=jnp.float32)
        copy = pltpu.make_async_copy(held.at[here], out.at[here], store.at[len(stores)])
        copy.start()
        stores.append(copy)

    for copy in loads[:2]:
        copy.wait()
    for at in range(0, fi, step):
        if at == step:
            loads[2].wait()
        block(0, at, du_img, g_img, grad_img)
    if fi <= step:
        loads[2].wait()
    loads[3].wait()
    for at in range(0, ft, step):
        block(fi, at, du_txt, g_txt, grad_txt)
    for copy in stores:
        copy.wait()


def whole_batch(n_img, n_txt, image_feats, text_feats, teacher_img, teacher_txt, proj_img, proj_txt):
    held = exchange(n_img, n_txt, image_feats, text_feats, teacher_img, teacher_txt, proj_img, proj_txt)
    (fi, ds), ft = proj_img.shape, proj_txt.shape[0]
    vmem = pl.BlockSpec(memory_space=pltpu.VMEM)
    hbm = pl.BlockSpec(memory_space=pltpu.HBM)
    f32 = jnp.float32
    loss, grad_img, grad_txt = pl.pallas_call(
        grads_kernel,
        out_shape=[
            jax.ShapeDtypeStruct((1, 1), f32),
            jax.ShapeDtypeStruct((fi, ds), f32),
            jax.ShapeDtypeStruct((ft, ds), f32),
        ],
        in_specs=[hbm] * 4,
        out_specs=[hbm] * 3,
        scratch_shapes=[pltpu.VMEM(h.shape, h.dtype) for h in held[1:]]
        + [
            pltpu.VMEM((fi, ds), f32),
            pltpu.VMEM((ft, ds), f32),
            pltpu.SemaphoreType.DMA((4,)),
            pltpu.SemaphoreType.DMA((1 + pl.cdiv(fi, LANES * 2) + pl.cdiv(ft, LANES * 2),)),
        ],
        compiler_params=pltpu.CompilerParams(vmem_limit_bytes=FUSED_VMEM_BYTES),
        name="weight_grads",
    )(*held)
    return (loss.reshape(()), grad_img, grad_txt)


def fits(n_img, n_txt, image, text, t_img, t_txt, proj_img, proj_txt):
    rows, fi = image.shape
    batch = rows * n_img * n_txt
    ft, dt, ds = text.shape[1], t_img.shape[1], proj_img.shape[1]
    half = (fi + ft) // 2
    held = 2 * batch * (fi + ft) + 12 * batch * ds + 16 * batch * batch + 6 * ds * (fi + ft)
    aligned = rows % 16 == 0 and rows * n_img == LANES and rows * n_txt * 2 <= LANES and ft % 128 == 0 and dt % 128 == 0
    aligned = aligned and fi % 128 == 0 and (fi + ft) % 256 == 0 and half < fi and (rows * n_txt) % 32 == 0
    return n_txt == 4 and n_img % 2 == 0 and n_img > 2 and aligned and held <= FUSED_VMEM_BYTES * 3 // 4


def solution(mesh):
    n_img, n_txt = mesh.shape["img"], mesh.shape["txt"]

    def per_device(*arrays):
        if fits(n_img, n_txt, *arrays):
            return whole_batch(n_img, n_txt, *arrays)
        return shards(*arrays)

    return jax.shard_map(
        per_device,
        mesh=mesh,
        in_specs=(
            P(("img", "txt"), None),
            P(("txt", "img"), None),
            P(("img", "txt"), None),
            P(("txt", "img"), None),
            P(),
            P(),
        ),
        out_specs=(P(), P(), P()),
        check_vma=False,
    )
```

```python
import functools

import jax
import jax.numpy as jnp
from jax import lax
from jax.experimental import pallas as pl
from jax.experimental.pallas import tpu as pltpu
from jax.sharding import PartitionSpec as P

EPS = 1e-06
TEACHER_SCALE = 100.0
STUDENT_SCALE = 50.0


def project(feats, weight):
    u = jnp.dot(feats, weight, preferred_element_type=jnp.float32)
    inv = lax.rsqrt(jnp.sum(u * u, axis=1, keepdims=True) + EPS)
    return (u * inv, inv)


def normed(raw):
    x = raw.astype(jnp.float32)
    return (x * lax.rsqrt(jnp.sum(x * x, axis=1, keepdims=True) + EPS)).astype(jnp.bfloat16)


def tangent(grad_rows, embeds, inverse):
    return (grad_rows - embeds * jnp.sum(embeds * grad_rows, 1, keepdims=True)) * inverse


def weight_grad(feats, du_rows):
    return lax.dot_general(
        feats.astype(jnp.float32),
        du_rows,
        (((0,), (0,)), ((), ())),
        precision=lax.Precision.HIGHEST,
    )


def tile_terms(block_q_img, block_q_txt, block_s_img, block_s_txt):
    tl = TEACHER_SCALE * jnp.dot(block_q_img, block_q_txt.T, preferred_element_type=jnp.float32)
    sl = STUDENT_SCALE * jnp.dot(block_s_img, block_s_txt.T, preferred_element_type=jnp.float32)
    rtm, rsm = lax.pmax((tl.max(1), sl.max(1)), "txt")
    rts, rss = lax.psum(
        (jnp.sum(jnp.exp(tl - rtm[:, None]), 1), jnp.sum(jnp.exp(sl - rsm[:, None]), 1)), "txt"
    )
    ctm, csm = lax.pmax((tl.max(0), sl.max(0)), "img")
    cts, css = lax.psum(
        (jnp.sum(jnp.exp(tl - ctm[None, :]), 0), jnp.sum(jnp.exp(sl - csm[None, :]), 0)), "img"
    )
    pt_row = jnp.exp(tl - rtm[:, None]) / rts[:, None]
    ps_row = jnp.exp(sl - rsm[:, None]) / rss[:, None]
    pt_col = jnp.exp(tl - ctm[None, :]) / cts[None, :]
    ps_col = jnp.exp(sl - csm[None, :]) / css[None, :]
    diff = tl - sl
    n_img = lax.axis_size("img")
    n_txt = lax.axis_size("txt")
    local_term = jnp.sum(pt_row * diff) + jnp.sum(pt_col * diff)
    local_term = local_term + jnp.sum(rsm + jnp.log(rss) - rtm - jnp.log(rts)) / n_txt
    local_term = local_term + jnp.sum(csm + jnp.log(css) - ctm - jnp.log(cts)) / n_img
    grad_tile = (0.5 * STUDENT_SCALE * (ps_row - pt_row + (ps_col - pt_col))).astype(jnp.bfloat16)
    part_img = jnp.dot(grad_tile, block_s_txt, preferred_element_type=jnp.float32)
    part_txt = lax.dot_general(
        grad_tile, block_s_img, (((0,), (0,)), ((), ())), preferred_element_type=jnp.float32
    )
    return (part_img, part_txt, local_term)


def shards(image_feats, text_feats, teacher_img, teacher_txt, proj_img, proj_txt):
    e_img, inv_img = project(image_feats, proj_img)
    e_txt, inv_txt = project(text_feats, proj_txt)
    q_img = normed(teacher_img)
    q_txt = normed(teacher_txt)
    feats_img, block_q_img = (
        lax.all_gather(image_feats, "txt", axis=0, tiled=True),
        lax.all_gather(q_img, "txt", axis=0, tiled=True),
    )
    feats_txt, block_q_txt = (
        lax.all_gather(text_feats, "img", axis=0, tiled=True),
        lax.all_gather(q_txt, "img", axis=0, tiled=True),
    )
    block_s_img = project(feats_img, proj_img)[0].astype(jnp.bfloat16)
    block_s_txt = project(feats_txt, proj_txt)[0].astype(jnp.bfloat16)
    part_img, part_txt, local_term = tile_terms(block_q_img, block_q_txt, block_s_img, block_s_txt)
    d_img = lax.psum_scatter(part_img, "txt", scatter_dimension=0, tiled=True)
    d_txt = lax.psum_scatter(part_txt, "img", scatter_dimension=0, tiled=True)
    local_img = weight_grad(image_feats, tangent(d_img, e_img, inv_img))
    local_txt = weight_grad(text_feats, tangent(d_txt, e_txt, inv_txt))
    grad_img, grad_txt, total = lax.psum((local_img, local_txt, local_term), ("img", "txt"))
    batch_total = image_feats.shape[0] * lax.axis_size("img") * lax.axis_size("txt")
    loss = total / (2.0 * batch_total)
    return (loss, grad_img, grad_txt)


MESH = pl.DeviceIdType.MESH
FUSED_VMEM_BYTES = 60 * 1024 * 1024
LANES = 128


def dot_nt(a, b):
    return lax.dot_general(a, b, (((1,), (1,)), ((), ())), preferred_element_type=jnp.float32)


def dot_tn(a, b):
    return lax.dot_general(a, b, (((0,), (0,)), ((), ())), preferred_element_type=jnp.float32)


class LineSpread:
    def __init__(self, place, buf, halves, sems, log, straight=False):
        self.place, self.buf, self.halves, self.log, self.straight = place, buf, halves, log, straight
        self.sz, self.rz, self.sl, self.rl, self.sc, self.rc = sems

    def copy(self, at, part, peer, ssem, rsem):
        if part is None:
            ref = self.buf.at[at]
        else:
            lo, hi = self.halves[part]
            ref = self.buf.at[at, lo:hi]
        return pltpu.make_async_remote_copy(
            src_ref=ref, dst_ref=ref, send_sem=ssem, recv_sem=rsem, device_id=peer, device_id_type=MESH
        )

    def send(self, *args):
        copy = self.copy(*args)
        copy.start()
        self.log.append(copy)

    def arrived(self, at, part, ssem, rsem):
        self.copy(at, part, self.place.partner, ssem, rsem).wait_recv()

    def own_z(self):
        p = self.place
        for k in range(1, p.nz):
            self.send(p.slot(p.img, p.txt), None, p.z_peer(k), self.sz.at[k - 1], self.rz.at[k - 1])

    def line(self):
        p = self.place
        for k in range(1, p.nz):
            self.arrived(p.slot(p.source(k), p.txt), None, self.sz.at[k - 1], self.rz.at[k - 1])
        at = p.line(p.img, p.txt)
        if self.straight:
            self.send(at, None, (p.img, p.d_txt), self.sl.at[2], self.rl.at[2])
        self.send(at, None, (p.img, p.x_txt), self.sl.at[0], self.rl.at[0])
        self.send(at, None, (p.img, p.y_txt), self.sl.at[1], self.rl.at[1])
        self.send(at, None, p.partner, self.sc.at[0], self.rc.at[0])

    def turn(self):
        p = self.place
        for i, (near, far) in enumerate([(p.x_txt, p.y_txt), (p.y_txt, p.x_txt)]):
            at = p.line(p.img, near)
            self.arrived(at, None, self.sl.at[i], self.rl.at[i])
            if not self.straight:
                self.send(at, i, (p.img, far), self.sl.at[2 + i], self.rl.at[2 + i])
            self.send(at, None, p.partner, self.sc.at[1 + i], self.rc.at[1 + i])

    def last(self):
        p = self.place
        at = p.line(p.img, p.d_txt)
        for i, part in self.parts():
            self.arrived(at, part, self.sl.at[2 + i], self.rl.at[2 + i])
        self.send(at, None, p.partner, self.sc.at[3], self.rc.at[3])

    def parts(self):
        return ((0, None),) if self.straight else ((0, 0), (1, 1))

    def whole(self, which):
        p = self.place
        at = p.line(p.other, (p.txt, p.x_txt, p.y_txt, p.d_txt)[which])
        self.arrived(at, None, self.sc.at[which], self.rc.at[which])


class BlockSpread:
    def __init__(self, place, buf, halves, sems, log, straight=False):
        self.place, self.buf, self.halves, self.log, self.straight = place, buf, halves, log, straight
        self.sz, self.rz, self.sx, self.rx, self.sy, self.ry, self.sc, self.rc, self.sd, self.rd, self.se, self.re = sems

    def ref(self, at, part):
        if part is None:
            return self.buf.at[at]
        lo, hi = self.halves[part]
        return self.buf.at[at, lo:hi]

    def copy(self, at, part, peer, ssem, rsem):
        ref = self.ref(at, part)
        return pltpu.make_async_remote_copy(
            src_ref=ref, dst_ref=ref, send_sem=ssem, recv_sem=rsem, device_id=peer, device_id_type=MESH
        )

    def send(self, *args):
        copy = self.copy(*args)
        copy.start()
        self.log.append(copy)

    def arrived(self, at, part, ssem, rsem):
        self.copy(at, part, self.place.partner, ssem, rsem).wait_recv()

    def own_z(self):
        p = self.place
        for k in range(1, p.nz):
            self.send(p.slot(p.img, p.txt), None, p.z_peer(k), self.sz.at[k - 1], self.rz.at[k - 1])

    def line(self, k):
        p = self.place
        at = p.slot(p.source(k), p.txt)
        if k > 0:
            self.arrived(at, None, self.sz.at[k - 1], self.rz.at[k - 1])
        self.send(at, None, (p.img, p.x_txt), self.sx.at[k], self.rx.at[k])
        self.send(at, None, (p.img, p.y_txt), self.sy.at[k], self.ry.at[k])
        if self.straight:
            self.send(at, None, (p.img, p.d_txt), self.sd.at[0, k], self.rd.at[0, k])
        self.send(at, None, p.partner, self.sc.at[0, k], self.rc.at[0, k])

    def turn(self, k):
        p = self.place
        at = p.slot(p.source(k), p.x_txt)
        self.arrived(at, None, self.sx.at[k], self.rx.at[k])
        if not self.straight:
            self.send(at, 0, (p.img, p.y_txt), self.sd.at[0, k], self.rd.at[0, k])
        self.send(at, None, p.partner, self.sc.at[1, k], self.rc.at[1, k])
        at = p.slot(p.source(k), p.y_txt)
        self.arrived(at, None, self.sy.at[k], self.ry.at[k])
        if not self.straight:
            self.send(at, 1, (p.img, p.x_txt), self.sd.at[1, k], self.rd.at[1, k])
        self.send(at, None, p.partner, self.sc.at[2, k], self.rc.at[2, k])

    def last(self, k):
        p = self.place
        at = p.slot(p.source(k), p.d_txt)
        for i, part in self.parts():
            self.arrived(at, part, self.sd.at[i, k], self.rd.at[i, k])
            self.send(at, part, p.partner, self.se.at[i, k], self.re.at[i, k])

    def parts(self):
        return ((0, None),) if self.straight else ((0, 0), (1, 1))

    def whole(self, which):
        p = self.place
        for k in range(p.nz):
            source = p.other_source(k)
            if which < 3:
                at = p.slot(source, (p.txt, p.x_txt, p.y_txt)[which])
                self.arrived(at, None, self.sc.at[which, k], self.rc.at[which, k])
            else:
                for i, part in self.parts():
                    self.arrived(p.slot(source, p.d_txt), part, self.se.at[i, k], self.re.at[i, k])


class Place:
    def __init__(self, n_img, n_txt):
        self.n_img, self.n_txt, self.nz = n_img, n_txt, n_img // 2
        self.img, self.txt = lax.axis_index("img"), lax.axis_index("txt")
        self.other = self.img + 1 - 2 * lax.rem(self.img, 2)
        self.partner = (self.other, self.txt)
        self.x_txt = self.txt + 1 - 2 * lax.rem(self.txt, 2)
        self.y_txt = lax.rem(self.txt + 2, 4)
        self.d_txt = lax.rem(self.x_txt + 2, 4)

    def order(self, img):
        return lax.rem(img, 2) * self.nz + img // 2

    def slot(self, img, txt):
        return txt * self.n_img + self.order(img)

    def line(self, img, txt):
        return pl.ds(txt * self.n_img + lax.rem(img, 2) * self.nz, self.nz)

    def source(self, k):
        return lax.rem(self.img + self.n_img - 2 * k, self.n_img)

    def other_source(self, k):
        return lax.rem(self.other + self.n_img - 2 * k, self.n_img)

    def z_peer(self, k):
        return (lax.rem(self.img + 2 * k, self.n_img), self.txt)

    def img_at(self, k):
        return lax.rem(self.img + k, self.n_img)

    def txt_at(self, k):
        return lax.rem(self.txt + k, self.n_txt)


def exchange_kernel(n_img, n_txt, image, text, t_img, t_txt, p_img, p_txt, *refs):
    loss_out, turned_out, du_img_out, du_txt_out = refs[:4]
    feats, tiles, e_img, e_txt, i_img, i_txt, s_img, s_txt, sl, ps, du_img, du_txt = refs[4:16]
    turned, loss = refs[54:56]
    raw, q_img, q_txt, tile, row_st, col_st, w_img, w_txt, g_tile, load = refs[16:26]
    tz_s, tz_r, tc_s, tc_r, ti_s, ti_r, rs_s, rs_r, cs_s, cs_r = refs[26:36]
    f_sems, p_sems = refs[36:48], refs[48:54]
    p = Place(n_img, n_txt)
    nz, img, txt = p.nz, p.img, p.txt
    rows, fi = image.shape
    ft, dt = text.shape[1], t_img.shape[1]
    half = feats.shape[3]
    batch = sl.shape[0]
    mine = p.slot(img, txt)

    loads = [
        pltpu.make_async_copy(t_img, raw.at[0], load.at[0]),
        pltpu.make_async_copy(t_txt, raw.at[1], load.at[1]),
        pltpu.make_async_copy(image.at[:, 0:half], feats.at[mine, 0], load.at[2]),
        pltpu.make_async_copy(image.at[:, half:fi], feats.at[mine, 1, :, 0 : fi - half], load.at[3]),
        pltpu.make_async_copy(text, feats.at[mine, 1, :, fi - half : half], load.at[4]),
        pltpu.make_async_copy(p_img, w_img, load.at[5]),
        pltpu.make_async_copy(p_txt, w_txt, load.at[6]),
    ]
    for copy in loads:
        copy.start()
    peers = [(p.img_at(k), txt) for k in range(1, n_img)] + [(img, p.txt_at(k)) for k in range(1, n_txt)]
    barrier = pltpu.get_barrier_semaphore()
    for peer in peers:
        pl.semaphore_signal(barrier, inc=1, device_id=peer, device_id_type=MESH)
    loads[0].wait()
    q_img[txt] = normed(raw[0])
    loads[1].wait()
    mine_q = p.order(img)
    q_txt[mine_q] = normed(raw[1])
    for copy in loads[2:5]:
        copy.wait()
    pl.semaphore_wait(barrier, len(peers))

    log = []

    def copy_of(ref, peer, ssem, rsem):
        return pltpu.make_async_remote_copy(
            src_ref=ref, dst_ref=ref, send_sem=ssem, recv_sem=rsem, device_id=peer, device_id_type=MESH
        )

    def send(*args):
        copy = copy_of(*args)
        copy.start()
        log.append(copy)

    def arrived(ref, ssem, rsem):
        copy_of(ref, p.partner, ssem, rsem).wait_recv()

    f = BlockSpread(p, feats, ((0, 1), (1, 2)), f_sems, log)
    rows_in, cols_in = rows * n_txt, rows * n_img
    g = LineSpread(p, tiles, ((0, rows_in // 2), (rows_in // 2, rows_in + 16)), p_sems, log, straight=True)

    for k in range(1, nz):
        send(q_txt.at[mine_q], p.z_peer(k), tz_s.at[k - 1], tz_r.at[k - 1])
    for k in range(1, n_txt):
        send(q_img.at[txt], (img, p.txt_at(k)), ti_s.at[k - 1], ti_r.at[k - 1])
    f.line(0)
    for copy in log[: nz - 1]:
        copy.wait_send()
    del log[: nz - 1]
    f.own_z()
    f.turn(0)
    for k in range(1, nz):
        arrived(q_txt.at[p.order(p.source(k))], tz_s.at[k - 1], tz_r.at[k - 1])
    send(q_txt.at[p.line(img, 0)], p.partner, tc_s.at[0], tc_r.at[0])
    for k in range(1, n_txt):
        arrived(q_img.at[p.txt_at(n_txt - k)], ti_s.at[k - 1], ti_r.at[k - 1])
    arrived(q_txt.at[p.line(p.other, 0)], tc_s.at[0], tc_r.at[0])

    t = TEACHER_SCALE * dot_nt(q_img[...].reshape(rows_in, dt), q_txt[...].reshape(cols_in, dt))
    tile[...] = t
    m = jnp.max(t, axis=1, keepdims=True)
    s = jnp.sum(jnp.exp(t - m), axis=1, keepdims=True)
    lane = lax.broadcasted_iota(jnp.int32, (rows_in, cols_in), 1)
    packed = jnp.where(lane < rows_in, m, s).T
    row_st[txt] = jnp.zeros(row_st.shape[1:], jnp.float32)
    row_st[txt, 0:1, 0:rows_in] = packed[0:1, :]
    row_st[txt, 1:2, 0:rows_in] = packed[rows_in : rows_in + 1, :]
    m = jnp.max(t, axis=0, keepdims=True)
    col_st[img] = jnp.zeros(col_st.shape[1:], jnp.float32)
    col_st[img, 0:1, :] = m
    col_st[img, 1:2, :] = jnp.sum(jnp.exp(t - m), axis=0, keepdims=True)
    for k in range(1, n_img):
        send(col_st.at[img], (p.img_at(k), txt), cs_s.at[k - 1], cs_r.at[k - 1])
    for k in range(1, n_txt):
        send(row_st.at[txt], (img, p.txt_at(k)), rs_s.at[k - 1], rs_r.at[k - 1])

    for k in range(1, nz):
        f.line(k)
    for k in range(1, n_img):
        arrived(col_st.at[p.img_at(n_img - k)], cs_s.at[k - 1], cs_r.at[k - 1])
    for k in range(1, n_txt):
        arrived(row_st.at[p.txt_at(n_txt - k)], rs_s.at[k - 1], rs_r.at[k - 1])

    def log_sum(stats):
        m = jnp.max(stats[:, 0, :], axis=0, keepdims=True)
        return m + jnp.log(jnp.sum(stats[:, 1, :] * jnp.exp(stats[:, 0, :] - m), axis=0, keepdims=True))

    lz_row = log_sum(row_st[:, :, 0:rows_in])
    lz_col = log_sum(col_st[...])
    t = tile[...]
    both = jnp.exp(t - jnp.broadcast_to(lz_row, (cols_in, rows_in)).T) + jnp.exp(t - lz_col)
    part = jnp.sum(both * t, axis=0, keepdims=True) - lz_col / n_img
    part = part - jnp.sum(lz_row, axis=1, keepdims=True) / (n_txt * cols_in)
    high = part.astype(jnp.bfloat16).astype(jnp.float32)
    middle = (part - high).astype(jnp.bfloat16).astype(jnp.float32)
    line = lax.broadcasted_iota(jnp.int32, (16, cols_in), 0)
    pieces = jnp.where(line == 0, high, jnp.where(line == 1, middle, jnp.where(line == 2, part - high - middle, 0.0)))
    tiles[mine, 0:rows_in, :] = both.astype(jnp.bfloat16)
    tiles[mine, rows_in : rows_in + 16, :] = pieces.astype(jnp.bfloat16)
    g.own_z()

    def embed(j):
        at = pl.ds(pl.multiple_of(j * cols_in, cols_in), cols_in)
        here = pl.ds(j * n_img, n_img)
        rest = feats[here, 1].reshape(cols_in, half)
        x = jnp.concatenate([feats[here, 0].reshape(cols_in, half), rest[:, 0 : fi - half]], axis=1)
        turned[0:fi, at] = x.T
        turned[fi : fi + ft, at] = rest[:, fi - half : half].T
        e, inv = project(x, w_img[...])
        e_img[at, :], i_img[at, :] = e, inv
        s_img[at, :] = e.astype(jnp.bfloat16)
        e, inv = project(rest[:, fi - half : half], w_txt[...])
        e_txt[at, :], i_txt[at, :] = e, inv
        s_txt[at, :] = e.astype(jnp.bfloat16)

    for k in range(1, nz):
        f.turn(k)
    g.line()
    f.whole(0)
    for copy in loads[5:]:
        copy.wait()
    embed(txt)
    for k in range(nz):
        f.last(k)
    f.whole(1)
    embed(p.x_txt)
    f.whole(2)
    embed(p.y_txt)
    g.turn()
    g.last()
    f.whole(3)
    embed(p.d_txt)
    outs = [pltpu.make_async_copy(turned, turned_out, load.at[0])]
    outs[0].start()

    chunks = [slice(c * cols_in, (c + 1) * cols_in) for c in range(n_txt)]
    csm = jnp.full((1, batch), -jnp.inf, jnp.float32)
    total = jnp.zeros((1, 1), jnp.float32)
    for at in chunks:
        s = STUDENT_SCALE * dot_nt(s_img[at, :], s_txt[...])
        sl[at, :] = s
        m = jnp.max(s, axis=1, keepdims=True)
        es = jnp.exp(s - m)
        sums = jnp.sum(es, axis=1, keepdims=True)
        ps[at, :] = es * (1.0 / sums)
        total = total + jnp.sum(m + jnp.log(sums), axis=0, keepdims=True)
        csm = jnp.maximum(csm, jnp.max(s, axis=0, keepdims=True))
    css = jnp.zeros((1, batch), jnp.float32)
    for at in chunks:
        css = css + jnp.sum(jnp.exp(sl[at, :] - csm), axis=0, keepdims=True)
    lzc = csm + jnp.log(css)
    total = total + jnp.sum(lzc, axis=1, keepdims=True)
    for at in chunks:
        ps[at, :] = ps[at, :] + jnp.exp(sl[at, :] - lzc)
    for copy in log:
        copy.wait_send()
    for which in range(4):
        g.whole(which)

    def tile_rows(c):
        held = [tiles[i * n_img : (i + 1) * n_img, c * rows : (c + 1) * rows, :] for i in range(n_txt)]
        return jnp.concatenate([h.reshape(cols_in, cols_in) for h in held], axis=1).astype(jnp.float32)

    terms = jnp.zeros((1, batch), jnp.float32)
    for c, at in enumerate(chunks):
        pt = tile_rows(c)
        tile_g = (0.5 * STUDENT_SCALE * (ps[at, :] - pt)).astype(jnp.bfloat16)
        g_tile[at, :] = tile_g
        terms = terms - jnp.sum(pt * sl[at, :], axis=0, keepdims=True)
        d_img = jnp.dot(tile_g, s_txt[...], preferred_element_type=jnp.float32)
        du_img[at, :] = tangent(d_img, e_img[at, :], i_img[at, :]).astype(jnp.bfloat16)
    outs.append(pltpu.make_async_copy(du_img, du_img_out, load.at[1]))
    outs[1].start()
    parts = jnp.sum(tiles[:, rows_in : rows_in + 16, :].astype(jnp.float32), axis=0)
    total = total + jnp.sum(terms, axis=1, keepdims=True)
    total = total + jnp.sum(jnp.sum(parts, axis=0, keepdims=True), axis=1, keepdims=True)
    loss[...] = total / (2.0 * batch)
    outs.append(pltpu.make_async_copy(loss, loss_out, load.at[3]))
    outs[2].start()
    for at in chunks:
        d_txt = dot_tn(g_tile[:, at], s_img[...])
        du_txt[at, :] = tangent(d_txt, e_txt[at, :], i_txt[at, :]).astype(jnp.bfloat16)
    outs.append(pltpu.make_async_copy(du_txt, du_txt_out, load.at[2]))
    outs[3].start()
    for copy in outs:
        copy.wait()


def exchange(n_img, n_txt, image, text, t_img, t_txt, w_img, w_txt):
    rows, fi = image.shape
    ft, dt, ds = text.shape[1], t_img.shape[1], w_img.shape[1]
    nz, slots = n_img // 2, n_img * n_txt
    batch, rows_in, cols_in = rows * slots, rows * n_txt, rows * n_img
    f32, b16 = jnp.float32, jnp.bfloat16
    dma = pltpu.SemaphoreType.DMA
    vmem = pl.BlockSpec(memory_space=pltpu.VMEM)
    hbm = pl.BlockSpec(memory_space=pltpu.HBM)
    outs = [((1, 1), f32), ((fi + ft, batch), b16), ((batch, ds), b16), ((batch, ds), b16)]
    held = [
        ((slots, 2, rows, (fi + ft) // 2), b16),
        ((slots, rows_in + 16, cols_in), b16),
        ((batch, ds), f32),
        ((batch, ds), f32),
        ((batch, 1), f32),
        ((batch, 1), f32),
        ((batch, ds), b16),
        ((batch, ds), b16),
        ((batch, batch), f32),
        ((batch, batch), f32),
        ((batch, ds), b16),
        ((batch, ds), b16),
    ]
    scratch = [pltpu.VMEM(*h) for h in held] + [
        pltpu.VMEM((2, rows, dt), b16),
        pltpu.VMEM((n_txt, rows, dt), b16),
        pltpu.VMEM((n_img, rows, dt), b16),
        pltpu.VMEM((rows_in, cols_in), f32),
        pltpu.VMEM((n_txt, 8, LANES), f32),
        pltpu.VMEM((n_img, 8, LANES), f32),
        pltpu.VMEM((fi, ds), b16),
        pltpu.VMEM((ft, ds), b16),
        pltpu.VMEM((batch, batch), b16),
        dma((7,)),
    ]
    lines = [(nz - 1,), (4,), (4,)]
    blocks = [(nz - 1,), (nz,), (nz,), (3, nz), (2, nz), (2, nz)]
    for shape in [(nz - 1,), (1,), (n_txt - 1,), (n_txt - 1,), (n_img - 1,)] + blocks + lines:
        scratch += [dma(shape), dma(shape)]
    scratch += [pltpu.VMEM((fi + ft, batch), b16), pltpu.VMEM((1, 1), f32)]
    return pl.pallas_call(
        functools.partial(exchange_kernel, n_img, n_txt),
        out_shape=[jax.ShapeDtypeStruct(*s) for s in outs],
        in_specs=[hbm] * 6,
        out_specs=[hbm] * 4,
        scratch_shapes=scratch,
        compiler_params=pltpu.CompilerParams(
            collective_id=0, has_side_effects=True, vmem_limit_bytes=FUSED_VMEM_BYTES
        ),
        name="exchange_and_embed",
    )(image, text, t_img, t_txt, w_img, w_txt)


def grads_kernel(loss_in, turned_in, du_img_in, du_txt_in, loss, grad_img, grad_txt, turned, du_img, du_txt, g_img, g_txt, load, store):
    fi, ft = grad_img.shape[0], grad_txt.shape[0]
    step = LANES * 2
    loads = [
        pltpu.make_async_copy(du_img_in, du_img, load.at[0]),
        pltpu.make_async_copy(turned_in.at[0:step], turned.at[0:step], load.at[1]),
        pltpu.make_async_copy(turned_in.at[step : fi + ft], turned.at[step : fi + ft], load.at[2]),
        pltpu.make_async_copy(du_txt_in, du_txt, load.at[3]),
    ]
    for copy in loads:
        copy.start()
    stores = [pltpu.make_async_copy(loss_in, loss, store.at[0])]
    stores[0].start()

    def block(lo, at, du, held, out):
        rows = min(step, held.shape[0] - at)
        here = slice(at, at + rows)
        held[here, :] = jnp.dot(turned[lo + at : lo + at + rows, :], du[...], preferred_element_type=jnp.float32)
        copy = pltpu.make_async_copy(held.at[here], out.at[here], store.at[len(stores)])
        copy.start()
        stores.append(copy)

    for copy in loads[:2]:
        copy.wait()
    for at in range(0, fi, step):
        if at == step:
            loads[2].wait()
        block(0, at, du_img, g_img, grad_img)
    if fi <= step:
        loads[2].wait()
    loads[3].wait()
    for at in range(0, ft, step):
        block(fi, at, du_txt, g_txt, grad_txt)
    for copy in stores:
        copy.wait()


def whole_batch(n_img, n_txt, image_feats, text_feats, teacher_img, teacher_txt, proj_img, proj_txt):
    held = exchange(n_img, n_txt, image_feats, text_feats, teacher_img, teacher_txt, proj_img, proj_txt)
    (fi, ds), ft = proj_img.shape, proj_txt.shape[0]
    vmem = pl.BlockSpec(memory_space=pltpu.VMEM)
    hbm = pl.BlockSpec(memory_space=pltpu.HBM)
    f32 = jnp.float32
    loss, grad_img, grad_txt = pl.pallas_call(
        grads_kernel,
        out_shape=[
            jax.ShapeDtypeStruct((1, 1), f32),
            jax.ShapeDtypeStruct((fi, ds), f32),
            jax.ShapeDtypeStruct((ft, ds), f32),
        ],
        in_specs=[hbm] * 4,
        out_specs=[hbm] * 3,
        scratch_shapes=[pltpu.VMEM(h.shape, h.dtype) for h in held[1:]]
        + [
            pltpu.VMEM((fi, ds), f32),
            pltpu.VMEM((ft, ds), f32),
            pltpu.SemaphoreType.DMA((4,)),
            pltpu.SemaphoreType.DMA((1 + pl.cdiv(fi, LANES * 2) + pl.cdiv(ft, LANES * 2),)),
        ],
        compiler_params=pltpu.CompilerParams(vmem_limit_bytes=FUSED_VMEM_BYTES),
        name="weight_grads",
    )(*held)
    return (loss.reshape(()), grad_img, grad_txt)


def fits(n_img, n_txt, image, text, t_img, t_txt, proj_img, proj_txt):
    rows, fi = image.shape
    batch = rows * n_img * n_txt
    ft, dt, ds = text.shape[1], t_img.shape[1], proj_img.shape[1]
    half = (fi + ft) // 2
    held = 2 * batch * (fi + ft) + 12 * batch * ds + 16 * batch * batch + 6 * ds * (fi + ft)
    aligned = rows % 16 == 0 and rows * n_img == LANES and rows * n_txt * 2 <= LANES and ft % 128 == 0 and dt % 128 == 0
    aligned = aligned and fi % 128 == 0 and (fi + ft) % 256 == 0 and half < fi and (rows * n_txt) % 32 == 0
    return n_txt == 4 and n_img % 2 == 0 and n_img > 2 and aligned and held <= FUSED_VMEM_BYTES * 3 // 4


def solution(mesh):
    n_img, n_txt = mesh.shape["img"], mesh.shape["txt"]

    def per_device(*arrays):
        if fits(n_img, n_txt, *arrays):
            return whole_batch(n_img, n_txt, *arrays)
        return shards(*arrays)

    return jax.shard_map(
        per_device,
        mesh=mesh,
        in_specs=(
            P(("img", "txt"), None),
            P(("txt", "img"), None),
            P(("img", "txt"), None),
            P(("txt", "img"), None),
            P(),
            P(),
        ),
        out_specs=(P(), P(), P()),
        check_vma=False,
    )
```
